32 devices in a mesh: shard: 8 (over z, x), heads: 4 (over y, core).
Axes of the slice: x: 2, y: 2, z: 4, core: 2. Of those that a mesh axis runs over, the one named last changes fastest.
Arguments:
- tokens: bfloat16 [8192, 1024], P('shard', 'heads'), may hold values from -6 to 6
- z_weight: bfloat16 [1024, 2048], P('shard', 'heads'), may hold values from -0.1875 to 0.1875
- x_weight: bfloat16 [1024, 2048], P('shard', 'heads'), may hold values from -0.1875 to 0.1875
- bc_weight: bfloat16 [1024, 256], P('shard'), may hold values from -0.1875 to 0.1875
- dt_weight: bfloat16 [1024, 32], P('shard', 'heads'), may hold values from -0.1875 to 0.1875
- out_weight: bfloat16 [2048, 1024], P('heads', 'shard'), may hold values from -0.125 to 0.125
- norm_gain: float32 [1024], replicated, may hold values from 0.5 to 1.5
- gate_gain: float32 [2048], P('heads'), may hold values from 0.5 to 1.5
- x_conv_weight: float32 [4, 2048], P(None, 'heads'), may hold values from -3 to 3
- x_conv_bias: float32 [2048], P('heads'), may hold values from -3 to 3
- bc_conv_weight: float32 [4, 256], replicated, may hold values from -3 to 3
- bc_conv_bias: float32 [256], replicated, may hold values from -3 to 3
- step_bias: float32 [32], P('heads'), may hold values from -5 to -2
- decay_log: float32 [32], P('heads'), may hold values from -1 to 2.7
- skip_gain: float32 [32], P('heads'), may hold values from 0.5 to 1.5
- cotangent: bfloat16 [8192, 1024], P('shard', 'heads'), may hold values from -6 to 6
Outputs:
- mixed: bfloat16 [8192, 1024], P('shard', 'heads')
- tokens_grad: bfloat16 [8192, 1024], P('shard', 'heads')
- z_weight_grad: float32 [1024, 2048], P('shard', 'heads')
- x_weight_grad: float32 [1024, 2048], P('shard', 'heads')
- bc_weight_grad: float32 [1024, 256], P('shard', 'heads')
- dt_weight_grad: float32 [1024, 32], P('shard', 'heads')
- out_weight_grad: float32 [2048, 1024], P('heads', 'shard')
- norm_gain_grad: float32 [1024], P('heads')
- gate_gain_grad: float32 [2048], P('heads')
- x_conv_weight_grad: float32 [4, 2048], P(None, 'heads')
- x_conv_bias_grad: float32 [2048], P('heads')
- bc_conv_weight_grad: float32 [4, 256], replicated
- bc_conv_bias_grad: float32 [256], replicated
- step_bias_grad: float32 [32], P('heads')
- decay_log_grad: float32 [32], P('heads')
- skip_gain_grad: float32 [32], P('heads')
The draws below stay inside these ranges and needn't reach their ends.
All inputs are finite; a program needn't handle non-finite values.
Results may differ from the reference program's by a relative error of at most 0.0095.
Values may be sent and summed in bfloat16 or wider, within the bound.
No kernel may reach another device: no remote copies, remote signals or barrier semaphores. Data moves between devices by JAX's collectives and lax.ppermute only.
A program may use at most 128 MiB of HBM per device.

```python
import jax
import jax.numpy as jnp
from jax import lax

D = 1024
HEADS = 32
HEADDIM = 64
STATE = 128
CONV_WIDTH = 4
BLOCK_LEN = 256
LEN = 1024
INNER = 2048
TOKENS = 8192


def level_of(own_key, extent, shards, least, high):
    loudness, own = 1.0, jax.random.fold_in(own_key, 6)
    for axis_at, parts in shards:
        draws = jnp.exp(jax.random.uniform(jax.random.fold_in(own, axis_at), (parts,), jnp.float32, least / len(shards), high / len(shards)))
        loudness = loudness * jnp.repeat(draws, extent[axis_at] // parts).reshape([-1 if axis == axis_at else 1 for axis in range(len(extent))])
    return loudness


def gaussian(key, dims, width, limit, cuts=(), kind=jnp.bfloat16):
    values = jax.random.normal(key, dims, jnp.float32) * width
    if len(cuts) > 0:
        values = level_of(key, dims, cuts, -0.22, 0.18) * values
    return jnp.clip(values, min=-limit, max=limit).astype(kind)


def setup_inputs(seed: int = 0) -> dict:
    seeds = jax.random.split(jax.random.key(seed), 17)
    tokens = gaussian(seeds[0], (TOKENS, D), 1.0, 6.0, ((0, 8), (1, 4)))
    z_weight = gaussian(seeds[1], (D, INNER), D ** -0.5, 0.1875, ((0, 8), (1, 4)))
    x_weight = gaussian(seeds[2], (D, INNER), D ** -0.5, 0.1875, ((0, 8), (1, 4)))
    bc_weight = gaussian(seeds[3], (D, 2 * STATE), D ** -0.5, 0.1875, ((0, 8),))
    dt_weight = gaussian(seeds[4], (D, HEADS), D ** -0.5, 0.1875, ((0, 8), (1, 4)))
    out_weight = gaussian(seeds[5], (INNER, D), INNER ** -0.5, 0.125, ((0, 4), (1, 8)))
    norm_gain = jnp.clip(1.0 + 0.1 * jax.random.normal(seeds[6], (D,), jnp.float32), 0.5, 1.5)
    gate_gain = jnp.clip(1.0 + 0.1 * jax.random.normal(seeds[7], (INNER,), jnp.float32), 0.5, 1.5)
    x_conv_weight = gaussian(seeds[8], (CONV_WIDTH, INNER), CONV_WIDTH ** -0.5, 3.0, ((1, 4),), jnp.float32)
    x_conv_bias = gaussian(seeds[9], (INNER,), 0.5, 3.0, ((0, 4),), jnp.float32)
    bc_conv_weight = gaussian(seeds[10], (CONV_WIDTH, 2 * STATE), CONV_WIDTH ** -0.5, 3.0, (), jnp.float32)
    bc_conv_bias = gaussian(seeds[11], (2 * STATE,), 0.5, 3.0, (), jnp.float32)
    step_bias = jnp.clip(-5.0 + 3.0 * jax.random.uniform(seeds[12], (HEADS,), jnp.float32) ** level_of(seeds[12], (HEADS,), ((0, 4),), -0.2, 0.2), -5.0, -2.0)
    decay_log = jnp.clip(-1.0 + 3.7 * jax.random.uniform(seeds[13], (HEADS,), jnp.float32) ** level_of(seeds[13], (HEADS,), ((0, 4),), -0.2, 0.2), -1.0, 2.7)
    skip_gain = jnp.clip(0.5 + 1.0 * jax.random.uniform(seeds[14], (HEADS,), jnp.float32) ** level_of(seeds[14], (HEADS,), ((0, 4),), -0.2, 0.2), 0.5, 1.5)
    cotangent = gaussian(seeds[15], (TOKENS, D), 1.0, 6.0, ((0, 8), (1, 4)))
    return {"tokens": tokens, "z_weight": z_weight, "x_weight": x_weight, "bc_weight": bc_weight, "dt_weight": dt_weight, "out_weight": out_weight, "norm_gain": norm_gain, "gate_gain": gate_gain, "x_conv_weight": x_conv_weight, "x_conv_bias": x_conv_bias, "bc_conv_weight": bc_conv_weight, "bc_conv_bias": bc_conv_bias, "step_bias": step_bias, "decay_log": decay_log, "skip_gain": skip_gain, "cotangent": cotangent}


epsilon = 1e-05
highest = lax.Precision.HIGHEST

@jax.custom_vjp
def low(v):
    return lax.optimization_barrier(v.astype(jnp.bfloat16)).astype(jnp.float32)

@jax.custom_vjp
def low_back(v):
    return v

def low_keep(v):
    return (low(v), None)

def low_pass(kept, grad):
    return (grad,)

def back_keep(v):
    return (v, None)

def back_low(kept, grad):
    return (low(grad),)
low.defvjp(low_keep, low_pass)
low_back.defvjp(back_keep, back_low)

def conv_silu(values, weights, biases):
    length = values.shape[1]
    padded = jnp.pad(values, ((0, 0), (CONV_WIDTH - 1, 0), (0, 0)))
    summed = biases + weights[0] * padded[:, 0:length]
    for tap_index in range(1, CONV_WIDTH):
        summed = summed + weights[tap_index] * padded[:, tap_index:tap_index + length]
    return jax.nn.silu(summed)

def to_blocks(values):
    seq_count, length = (values.shape[0], values.shape[1])
    shaped = values.reshape((seq_count, length // BLOCK_LEN, BLOCK_LEN) + values.shape[2:])
    return jnp.moveaxis(shaped, 1, 0)

def scan_step(state, pieces, decay_rate, skip_gain):
    block_x, block_b, block_c, block_dt = pieces
    cumulative = jnp.cumsum(block_dt * decay_rate, axis=1)
    by_head = jnp.swapaxes(cumulative, 1, 2)
    lower = jnp.tril(jnp.ones((BLOCK_LEN, BLOCK_LEN), dtype=bool))
    spread = by_head[:, :, :, None] - by_head[:, :, None, :]
    decays = jnp.where(lower, jnp.exp(jnp.where(lower, spread, 0.0)), 0.0)
    scores = jnp.einsum('stn,sun->stu', block_c, block_b, precision=highest)
    mixing = decays * scores[:, None] * jnp.swapaxes(block_dt, 1, 2)[:, :, None, :]
    within = jnp.einsum('shtu,suhp->sthp', mixing, block_x, precision=highest)
    carried = jnp.einsum('shpn,stn->sthp', state, block_c, precision=highest) * jnp.exp(cumulative)[..., None]
    final = cumulative[:, -1]
    weights_in = jnp.exp(final[:, None, :] - cumulative) * block_dt
    updated = jnp.exp(final)[:, :, None, None] * state + jnp.einsum('suh,suhp,sun->shpn', weights_in, block_x, block_b, precision=highest)
    outputs = within + carried + skip_gain[:, None] * block_x
    return (updated, outputs)

def state_space(inputs_x, inputs_b, inputs_c, steps_dt, decay_rate, skip_gain):
    seq_count, length, head_count, head_size = inputs_x.shape
    initial = jnp.zeros((seq_count, head_count, head_size, inputs_b.shape[-1]), jnp.float32)

    def stepper(state, pieces):
        return scan_step(state, pieces, decay_rate, skip_gain)
    ignored, results = lax.scan(jax.checkpoint(stepper), initial, (to_blocks(inputs_x), to_blocks(inputs_b), to_blocks(inputs_c), to_blocks(steps_dt)))
    return jnp.moveaxis(results, 0, 1).reshape(inputs_x.shape)

def forward(rows_in, z_weight, x_weight, bc_weight, dt_weight, out_weight, norm_gain, gate_gain, x_conv_weight, x_conv_bias, bc_conv_weight, bc_conv_bias, step_bias, decay_log, skip_gain):
    seq_count = rows_in.shape[0] // LEN
    scale_in = lax.rsqrt(lax.optimization_barrier(jnp.mean(rows_in * rows_in, axis=-1, keepdims=True)) + epsilon)
    normed = low(rows_in * scale_in * norm_gain)
    gate_in = low_back(jnp.dot(normed, z_weight, precision=highest))
    inner_in = low_back(jnp.dot(normed, x_weight, precision=highest))
    state_in = low_back(jnp.dot(normed, bc_weight, precision=highest))
    step_in = low_back(jnp.dot(normed, dt_weight, precision=highest))
    inner_conv = low(conv_silu(inner_in.reshape(seq_count, LEN, HEADS * HEADDIM), x_conv_weight, x_conv_bias))
    state_conv = low(conv_silu(state_in.reshape(seq_count, LEN, 2 * STATE), bc_conv_weight, bc_conv_bias))
    steps_dt = jax.nn.softplus(step_in.reshape(seq_count, LEN, HEADS) + step_bias)
    scanned = state_space(inner_conv.reshape(seq_count, LEN, HEADS, HEADDIM), state_conv[..., :STATE], state_conv[..., STATE:], steps_dt, -jnp.exp(decay_log), skip_gain)
    mixed_in = scanned.reshape(rows_in.shape[0], HEADS * HEADDIM) * jax.nn.silu(gate_in)
    scale_mid = lax.rsqrt(lax.optimization_barrier(jnp.mean(mixed_in * mixed_in, axis=-1, keepdims=True)) + epsilon)
    normed_mid = low(mixed_in * scale_mid * gate_gain)
    return rows_in + jnp.dot(normed_mid, out_weight, precision=highest)

def reference(tokens, z_weight, x_weight, bc_weight, dt_weight, out_weight, norm_gain, gate_gain, x_conv_weight, x_conv_bias, bc_conv_weight, bc_conv_bias, step_bias, decay_log, skip_gain, cotangent):
    params = tuple((item.astype(jnp.float32) for item in (z_weight, x_weight, bc_weight, dt_weight, out_weight, norm_gain, gate_gain, x_conv_weight, x_conv_bias, bc_conv_weight, bc_conv_bias, step_bias, decay_log, skip_gain)))
    seq_total = TOKENS // LEN
    group_size = 4 if seq_total % 4 == 0 else 1
    group_rows = group_size * LEN
    rows_grouped = tokens.reshape(seq_total // group_size, group_rows, D)
    cot_grouped = cotangent.reshape(seq_total // group_size, group_rows, D)

    def one_group(totals, pieces):
        rows_in, cot_in = pieces
        result, backward = jax.vjp(forward, rows_in.astype(jnp.float32), *params)
        grads = backward(cot_in.astype(jnp.float32))
        totals = tuple((running + addend for running, addend in zip(totals, grads[1:])))
        return (totals, (result.astype(jnp.bfloat16), grads[0].astype(jnp.bfloat16)))
    initial = tuple((jnp.zeros_like(item) for item in params))
    totals, (outputs, input_grads) = lax.scan(one_group, initial, (rows_grouped, cot_grouped))
    return (outputs.reshape(TOKENS, D), input_grads.reshape(TOKENS, D), totals[0], totals[1], totals[2], totals[3], totals[4], totals[5], totals[6], totals[7], totals[8], totals[9], totals[10], totals[11], totals[12], totals[13])
```

```python
import functools

import jax
import jax.numpy as jnp
from jax import lax
from jax.experimental import pallas as pl
from jax.experimental.pallas import tpu as pltpu
from jax.sharding import PartitionSpec as P

CONV_WIDTH = 4
LEN = 1024
BLOCK = 256
LANES = 128

epsilon = 1e-05
highest = lax.Precision.HIGHEST
f32 = jnp.float32
bf16 = jnp.bfloat16
VMEM_LIMIT = 50 * 1024 * 1024


def dot(left, right, left_dim=1, right_dim=0, precision=None):
    return lax.dot_general(
        left,
        right,
        (((left_dim,), (right_dim,)), ((), ())),
        precision=precision,
        preferred_element_type=f32,
    )


def spreader(head_share, head_size):
    row = lax.broadcasted_iota(jnp.int32, (LANES, head_share * head_size), 0)
    head = lax.broadcasted_iota(jnp.int32, (LANES, head_share * head_size), 1) // head_size
    return (row == head).astype(f32)


def lower_mask(size):
    row = lax.broadcasted_iota(jnp.int32, (size, size), 0)
    col = lax.broadcasted_iota(jnp.int32, (size, size), 1)
    return row >= col


def forward_kernel(
    sizes,
    rows_ref,
    gain_ref,
    weight_ref,
    x_taps_ref,
    x_bias_ref,
    s_taps_ref,
    s_bias_ref,
    step_bias_ref,
    rate_ref,
    skip_ref,
    normed_ref,
    inner_ref,
    x_pre_ref,
    x_ref,
    state_in_ref,
    s_pre_ref,
    bc_ref,
    step_ref,
    cum_ref,
    start_ref,
    scanned_ref,
    x_buf,
    s_buf,
    state,
):
    head_share, head_size, blocks_per_seq = sizes
    inner = head_share * head_size
    half = s_bias_ref.shape[1] // 2

    @pl.when(pl.program_id(0) % blocks_per_seq == 0)
    def _():
        x_buf[0:8, :] = jnp.zeros((8, inner), f32)
        s_buf[0:8, :] = jnp.zeros((8, 2 * half), f32)
        state[...] = jnp.zeros(state.shape, f32)

    rows = rows_ref[...].astype(f32)
    scale = lax.rsqrt(jnp.mean(rows * rows, axis=-1, keepdims=True) + epsilon)
    normed = (rows * scale * gain_ref[...]).astype(bf16)
    normed_ref[...] = normed
    projected = dot(normed, weight_ref[...])
    inner_in = projected[:, :inner]
    state_in = projected[:, inner : inner + 2 * half]
    step_pre = projected[:, inner + 2 * half :] + step_bias_ref[...]
    inner_ref[...] = inner_in
    state_in_ref[...] = state_in
    step_ref[...] = step_pre

    def conv(buf, values, taps_ref, bias_ref):
        buf[8 : 8 + BLOCK, :] = values
        total = bias_ref[...] + taps_ref[3:4, :] * values
        for tap in range(CONV_WIDTH - 1):
            total = total + taps_ref[tap : tap + 1, :] * buf[5 + tap : 5 + tap + BLOCK, :]
        buf[0:8, :] = buf[BLOCK : BLOCK + 8, :]
        return total

    x_pre = conv(x_buf, inner_in, x_taps_ref, x_bias_ref)
    x_pre_ref[...] = x_pre
    x = (x_pre * jax.nn.sigmoid(x_pre)).astype(bf16)
    x_ref[...] = x
    s_pre = conv(s_buf, state_in, s_taps_ref, s_bias_ref)
    s_pre_ref[...] = s_pre
    bc = (s_pre * jax.nn.sigmoid(s_pre)).astype(bf16)
    bc_ref[...] = bc
    b, c = bc[:, :half], bc[:, half:]

    steps = jax.nn.softplus(step_pre)
    lower = lower_mask(BLOCK)
    cum = dot(lower.astype(f32), steps * rate_ref[...], precision=highest)
    cum_ref[...] = cum
    cum_t = cum.T
    spread = spreader(head_share, head_size)
    cum_x = dot(cum, spread, precision=highest)
    steps_x = dot(steps, spread, precision=highest)
    last = cum_x[BLOCK - 1 :, :]
    x_f32 = x.astype(f32)
    stepped = x_f32 * steps_x
    stepped_low = stepped.astype(bf16)

    old = state[...]
    old_low = old.astype(bf16)
    start_ref[0] = old
    out = dot(c, old_low) * jnp.exp(cum_x) + skip_ref[...] * x_f32
    weighted = (stepped * jnp.exp(last - cum_x)).astype(bf16)
    state[...] = old * jnp.exp(last) + dot(b, weighted, 0, 0)

    scores = dot(c, b, 1, 1)
    pair = LANES // head_size
    lane_head = lax.broadcasted_iota(jnp.int32, (BLOCK, LANES), 1) // head_size
    for first in range(0, head_share, pair):
        at = first * head_size
        values = stepped_low[:, at : at + LANES]
        total = None
        for k in range(pair):
            head = first + k
            decays = jnp.exp(
                jnp.where(lower, cum[:, head : head + 1] - cum_t[head : head + 1, :], -1e30)
            )
            term = dot((decays * scores).astype(bf16), values)
            total = term if k == 0 else jnp.where(lane_head == k, term, total)
        scanned_ref[:, at : at + LANES] = out[:, at : at + LANES] + total


def forward_scan(rows, gain, weight, x_taps, x_bias, s_taps, s_bias, step_bias, rate, skip, head_share, head_size):
    count, features = rows.shape
    inner = head_share * head_size
    state2 = s_bias.shape[1]
    blocks = count // BLOCK
    whole = lambda a: pl.BlockSpec(a.shape, lambda i: (0,) * a.ndim)
    per = lambda width: pl.BlockSpec((BLOCK, width), lambda i: (i, 0))
    shape = lambda width, kind: jax.ShapeDtypeStruct((count, width), kind)
    outs = [
        (features, bf16),
        (inner, f32),
        (inner, f32),
        (inner, bf16),
        (state2, f32),
        (state2, f32),
        (state2, bf16),
        (LANES, f32),
        (LANES, f32),
    ]
    consts = (gain, weight, x_taps, x_bias, s_taps, s_bias, step_bias, rate, skip)
    return pl.pallas_call(
        functools.partial(forward_kernel, (head_share, head_size, LEN // BLOCK)),
        grid=(blocks,),
        in_specs=[per(features)] + [whole(a) for a in consts],
        out_specs=[per(w) for w, _ in outs]
        + [pl.BlockSpec((1, state2 // 2, inner), lambda i: (i, 0, 0)), per(inner)],
        out_shape=[shape(w, k) for w, k in outs]
        + [jax.ShapeDtypeStruct((blocks, state2 // 2, inner), f32), shape(inner, f32)],
        scratch_shapes=[
            pltpu.VMEM((BLOCK + 8, inner), f32),
            pltpu.VMEM((BLOCK + 8, state2), f32),
            pltpu.VMEM((state2 // 2, inner), f32),
        ],
        compiler_params=pltpu.CompilerParams(vmem_limit_bytes=VMEM_LIMIT),
    )(rows, *consts)


def backward_kernel(
    sizes,
    grad_ref,
    inner_ref,
    x_pre_ref,
    x_ref,
    bc_ref,
    step_ref,
    cum_ref,
    start_ref,
    x_taps_ref,
    rate_ref,
    skip_ref,
    grad_inner_ref,
    grad_bc_ref,
    grad_step_ref,
    sums_ref,
    small_ref,
    pre_buf,
    state,
):
    head_share, head_size, blocks_per_seq = sizes
    inner = head_share * head_size
    half = bc_ref.shape[1] // 2
    at_block = pl.num_programs(0) - 1 - pl.program_id(0)

    @pl.when(pl.program_id(0) == 0)
    def _():
        sums_ref[...] = jnp.zeros(sums_ref.shape, f32)
        small_ref[...] = jnp.zeros(small_ref.shape, f32)

    @pl.when(at_block % blocks_per_seq == blocks_per_seq - 1)
    def _():
        pre_buf[BLOCK:, :] = jnp.zeros((8, inner), f32)
        state[...] = jnp.zeros(state.shape, f32)

    grad = grad_ref[...]
    grad_low = grad.astype(bf16)
    x = x_ref[...].astype(f32)
    bc = bc_ref[...]
    b, c = bc[:, :half], bc[:, half:]
    step_pre = step_ref[...]
    steps = jax.nn.softplus(step_pre)
    cum = cum_ref[...]
    cum_t = cum.T
    lower = lower_mask(BLOCK)
    upper_low = jnp.logical_not(lower).astype(bf16)
    row = lax.broadcasted_iota(jnp.int32, (BLOCK, BLOCK), 0)
    col = lax.broadcasted_iota(jnp.int32, (BLOCK, BLOCK), 1)
    upper_incl = (row <= col).astype(bf16)
    strict = row > col
    spread = spreader(head_share, head_size)
    cum_x = dot(cum, spread, precision=highest)
    steps_x = dot(steps, spread, precision=highest)
    last = cum_x[BLOCK - 1 :, :]
    decay_in = jnp.exp(cum_x)
    decay_out = jnp.exp(last - cum_x)
    stepped = x * steps_x
    stepped_low = stepped.astype(bf16)

    old = start_ref[0]
    later = state[...]
    later_low = later.astype(bf16)
    grad_decayed = grad * decay_in
    grad_decayed_low = grad_decayed.astype(bf16)
    from_later = dot(b, later_low) * decay_out
    carried = dot(c, old.astype(bf16))
    grad_c = dot(grad_decayed_low, old.astype(bf16), 1, 1)
    grad_b = dot((stepped * decay_out).astype(bf16), later_low, 1, 1)
    state[...] = later * jnp.exp(last) + dot(c, grad_decayed_low, 0, 0)

    scores = dot(c, b, 1, 1)
    pair = LANES // head_size
    lane_head = lax.broadcasted_iota(jnp.int32, (BLOCK, LANES), 1) // head_size
    lane = lax.broadcasted_iota(jnp.int32, (BLOCK, LANES), 1)
    crossing = jnp.zeros((BLOCK, LANES), f32)
    gathered = jnp.zeros((BLOCK, BLOCK), f32)
    within = []
    for first in range(0, head_share, pair):
        at = first * head_size
        grads = grad_low[:, at : at + LANES]
        values = stepped_low[:, at : at + LANES]
        total = None
        for k in range(pair):
            head = first + k
            decays = jnp.exp(
                jnp.where(lower, cum[:, head : head + 1] - cum_t[head : head + 1, :], -1e30)
            )
            own = jnp.where(lane_head == k, grads, jnp.zeros_like(grads))
            products = dot(own, values, 1, 1) * decays
            gathered = gathered + products
            term = dot((decays * scores).astype(bf16), grads, 0, 0)
            total = term if k == 0 else jnp.where(lane_head == k, term, total)
            pairs = dot(upper_incl, (products * scores).astype(bf16))
            crossed = jnp.sum(jnp.where(strict, pairs, 0.0), axis=1, keepdims=True)
            crossing = jnp.where(lane == head, crossed, crossing)
        within.append(total)
    gathered_low = gathered.astype(bf16)
    grad_bc_ref[:, :half] = grad_b + dot(gathered_low, c, 0, 0)
    grad_bc_ref[:, half:] = grad_c + dot(gathered_low, b)

    by_x = jnp.concatenate(within, axis=1) + from_later
    fold = lambda values: dot(values, spread, 1, 1, precision=highest)
    direct = fold(by_x * x)
    into = fold(grad_decayed * carried)
    onward = steps * fold(from_later * x)
    tops = jnp.sum(later * old, axis=0, keepdims=True) * jnp.exp(last)
    spanning = fold(jnp.broadcast_to(tops, (8, inner)))[0:1, :]
    suffix = dot(upper_incl.astype(f32), into, precision=highest)
    prefix = dot(strict.astype(f32), onward, precision=highest)
    by_decay = crossing + suffix + prefix + spanning
    by_step = direct + rate_ref[...] * by_decay
    grad_step = by_step * jax.nn.sigmoid(step_pre)
    grad_step_ref[...] = grad_step.astype(bf16)
    small_ref[0:1, :] += jnp.sum(grad_step, axis=0, keepdims=True)
    small_ref[1:2, :] += jnp.sum(steps * by_decay, axis=0, keepdims=True)
    skips = jnp.sum(grad * x, axis=0, keepdims=True)
    small_ref[2:3, :] += fold(jnp.broadcast_to(skips, (8, inner)))[0:1, :]

    by_conv = steps_x * by_x + skip_ref[...] * grad
    x_pre = x_pre_ref[...]
    sig = jax.nn.sigmoid(x_pre)
    by_pre = by_conv * (sig * (1.0 + x_pre * (1.0 - sig)))
    pre_buf[0:BLOCK, :] = by_pre
    inner_in = inner_ref[...]
    grad_inner = x_taps_ref[3:4, :] * by_pre
    sums_ref[3:4, :] += jnp.sum(by_pre * inner_in, axis=0, keepdims=True)
    sums_ref[4:5, :] += jnp.sum(by_pre, axis=0, keepdims=True)
    for tap in range(CONV_WIDTH - 1):
        ahead = CONV_WIDTH - 1 - tap
        moved = pre_buf[ahead : ahead + BLOCK, :]
        grad_inner = grad_inner + x_taps_ref[tap : tap + 1, :] * moved
        sums_ref[tap : tap + 1, :] += jnp.sum(moved * inner_in, axis=0, keepdims=True)
    pre_buf[BLOCK:, :] = by_pre[0:8, :]
    grad_inner_ref[...] = grad_inner.astype(bf16)


def backward_scan(grad, inner_in, x_pre, x, bc, step_pre, cum, starts, x_taps, rate, skip, head_share, head_size):
    count, inner = grad.shape
    state2 = bc.shape[1]
    blocks = count // BLOCK
    whole = lambda a: pl.BlockSpec(a.shape, lambda i: (0,) * a.ndim)
    per = lambda width: pl.BlockSpec((BLOCK, width), lambda i: (blocks - 1 - i, 0))
    rows = (grad, inner_in, x_pre, x, bc, step_pre, cum)
    consts = (x_taps, rate, skip)
    fixed = lambda width: pl.BlockSpec((8, width), lambda i: (0, 0))
    return pl.pallas_call(
        functools.partial(backward_kernel, (head_share, head_size, LEN // BLOCK)),
        grid=(blocks,),
        in_specs=[per(a.shape[1]) for a in rows]
        + [pl.BlockSpec((1, state2 // 2, inner), lambda i: (blocks - 1 - i, 0, 0))]
        + [whole(a) for a in consts],
        out_specs=[per(inner), per(state2), per(LANES), fixed(inner), fixed(LANES)],
        out_shape=[
            jax.ShapeDtypeStruct((count, inner), bf16),
            jax.ShapeDtypeStruct((count, state2), f32),
            jax.ShapeDtypeStruct((count, LANES), bf16),
            jax.ShapeDtypeStruct((8, inner), f32),
            jax.ShapeDtypeStruct((8, LANES), f32),
        ],
        scratch_shapes=[
            pltpu.VMEM((BLOCK + 8, inner), f32),
            pltpu.VMEM((state2 // 2, inner), f32),
        ],
        compiler_params=pltpu.CompilerParams(vmem_limit_bytes=VMEM_LIMIT),
    )(*rows, starts, *consts)


def swap(value, axis, step):
    count = lax.axis_size(axis)
    return lax.ppermute(value, axis, [(i, i ^ step) for i in range(count)])


def steps_of(axis):
    count = lax.axis_size(axis)
    found = []
    while count > 1:
        count //= 2
        found.append(count)
    return found


def gather(value, axis, order):
    me = lax.axis_index(axis)
    held, done = value, []
    for step in order:
        got = swap(held, axis, step)
        bit = (me // step) % 2
        place = sum(1 for d in done if d > step)
        low = jnp.stack([held, got], axis=place)
        high = jnp.stack([got, held], axis=place)
        held = jnp.where(bit == 0, low, high)
        done.append(step)
    return held.reshape((-1,) + value.shape)


def reduce_scatter(value, axis, order):
    me = lax.axis_index(axis)
    left = sorted(order, reverse=True)
    held = value.reshape((2,) * len(left) + value.shape[1:])
    for step in order:
        place = left.index(step)
        bit = (me // step) % 2
        keep = lax.dynamic_index_in_dim(held, bit, place, keepdims=False)
        send = lax.dynamic_index_in_dim(held, 1 - bit, place, keepdims=False)
        got = swap(send.astype(bf16), axis, step)
        held = keep.astype(f32) + got.astype(f32)
        left.pop(place)
    return held


def all_sum(value, axis, order):
    for step in order:
        value = value + swap(value, axis, step)
    return value


def body(
    tokens,
    z_weight,
    x_weight,
    bc_weight,
    dt_weight,
    out_weight,
    norm_gain,
    gate_gain,
    x_conv_weight,
    x_conv_bias,
    bc_conv_weight,
    bc_conv_bias,
    step_bias,
    decay_log,
    skip_gain,
    cotangent,
):
    head_index = lax.axis_index("heads")
    head_groups = lax.axis_size("heads")
    shards = lax.axis_size("shard")
    row_count, feature_share = tokens.shape
    feature_total = feature_share * head_groups
    weight_rows, inner_share = z_weight.shape
    inner_total = inner_share * head_groups
    head_share = dt_weight.shape[1]
    head_size = inner_share // head_share
    state_width = bc_weight.shape[1]
    state_share = state_width // head_groups
    seq_count = row_count // LEN
    far = steps_of("shard")
    near = far[::-1]
    heads_far = steps_of("heads")
    heads_near = heads_far[::-1]

    step_pad = LANES - head_share
    scan_weight = jnp.concatenate(
        [x_weight, bc_weight, jnp.pad(dt_weight, ((0, 0), (0, step_pad)))], axis=1
    )
    rows_parts = gather(tokens, "heads", heads_far)
    full_rows = jnp.swapaxes(rows_parts, 0, 1).reshape(row_count, feature_total)
    whole_scan = gather(scan_weight, "shard", far).reshape(feature_total, -1)
    whole_z = gather(z_weight, "shard", far).reshape(feature_total, inner_share)
    whole_out = gather(out_weight.T, "shard", far).reshape(feature_total, inner_share)
    cot_parts = gather(cotangent, "heads", heads_far)
    full_cot = jnp.swapaxes(cot_parts, 0, 1).reshape(row_count, feature_total)

    pad_lanes = lambda v: jnp.pad(v, (0, step_pad))[None]
    rate = pad_lanes(-jnp.exp(decay_log))
    skip_x = jnp.repeat(skip_gain, head_size)[None]
    normed, inner_in, x_pre, x, state_in, s_pre, bc, step_pre, cum, starts, scanned = forward_scan(
        full_rows,
        norm_gain[None],
        whole_scan,
        x_conv_weight,
        x_conv_bias[None],
        bc_conv_weight,
        bc_conv_bias[None],
        pad_lanes(step_bias),
        rate,
        skip_x,
        head_share,
        head_size,
    )

    gate_in = dot(normed, whole_z)
    gate_sig = jax.nn.sigmoid(gate_in)
    gate_act = gate_in * gate_sig
    mixed_in = scanned * gate_act
    grad_mid = dot(full_cot, whole_out)
    grad_hat = grad_mid * gate_gain
    stats = all_sum(
        jnp.stack([jnp.sum(mixed_in * mixed_in, axis=-1), jnp.sum(grad_hat * mixed_in, axis=-1)]),
        "heads",
        heads_near,
    )
    scale_mid = lax.rsqrt(stats[0] / inner_total + epsilon)[:, None]
    mid_stat = scale_mid * stats[1][:, None]
    mid_hat = mixed_in * scale_mid
    normed_mid = (mid_hat * gate_gain).astype(bf16)
    gate_gain_grad = jnp.sum(mid_hat * grad_mid, axis=0)
    grad_mixed = scale_mid * (grad_hat - mid_hat * (mid_stat / inner_total))
    grad_scanned = grad_mixed * gate_act
    grad_gate = (grad_mixed * scanned * gate_sig * (1.0 + gate_in * (1.0 - gate_sig))).astype(bf16)

    early = jnp.concatenate([dot(normed, grad_gate, 0, 0), dot(full_cot, normed_mid, 0, 0)], axis=1)
    early_sum = reduce_scatter(
        early.astype(bf16).reshape(shards, weight_rows, 2 * inner_share), "shard", near
    )
    out_parts = dot(normed_mid, whole_out, 1, 1).astype(bf16)
    out_parts = jnp.swapaxes(out_parts.reshape(row_count, head_groups, feature_share), 0, 1)
    out_share = reduce_scatter(out_parts, "heads", heads_near)
    mixed = (tokens.astype(f32) + out_share).astype(bf16)

    grad_inner, grad_bc, grad_step, sums, small = backward_scan(
        grad_scanned,
        inner_in,
        x_pre,
        x,
        bc,
        step_pre,
        cum,
        starts,
        x_conv_weight,
        rate,
        skip_x,
        head_share,
        head_size,
    )

    state_start = head_index * state_share
    cut = lambda v: lax.dynamic_slice_in_dim(v, state_start, state_share, 1)
    bc_parts = jnp.swapaxes(grad_bc.astype(bf16).reshape(row_count, head_groups, state_share), 0, 1)
    bc_total = reduce_scatter(bc_parts, "heads", heads_near)
    own_pre = cut(s_pre)
    own_sig = jax.nn.sigmoid(own_pre)
    by_pre = bc_total * (own_sig * (1.0 + own_pre * (1.0 - own_sig)))
    by_seq = by_pre.reshape(seq_count, LEN, state_share)
    own_in = cut(state_in).reshape(seq_count, LEN, state_share)
    taps = cut(bc_conv_weight)
    ahead = jnp.pad(by_seq, ((0, 0), (0, CONV_WIDTH - 1), (0, 0)))
    grad_state = 0.0
    tap_grads = []
    for tap in range(CONV_WIDTH):
        at = CONV_WIDTH - 1 - tap
        moved = ahead[:, at : at + LEN]
        grad_state = grad_state + taps[tap] * moved
        tap_grads.append(jnp.sum(moved * own_in, axis=(0, 1)))
    tap_grads.append(jnp.sum(by_seq, axis=(0, 1)))
    grad_state = grad_state.reshape(row_count, state_share).astype(bf16)
    own_taps = lax.dynamic_update_slice(
        jnp.zeros((CONV_WIDTH + 1, state_width), f32), jnp.stack(tap_grads), (0, state_start)
    )

    grad_late = jnp.concatenate([grad_inner, grad_state, grad_step[:, :head_share]], axis=1)
    weight_late = jnp.concatenate(
        [
            whole_scan[:, :inner_share],
            lax.dynamic_slice_in_dim(whole_scan, inner_share + state_start, state_share, 1),
            whole_scan[:, inner_share + state_width : inner_share + state_width + head_share],
        ],
        axis=1,
    )
    late_sum = reduce_scatter(
        dot(normed, grad_late, 0, 0).astype(bf16).reshape(shards, weight_rows, -1), "shard", near
    )
    grad_normed = dot(grad_gate, whole_z, 1, 1) + dot(grad_late, weight_late, 1, 1)
    rows_f32 = full_rows.astype(f32)
    scale_in = lax.rsqrt(jnp.mean(rows_f32 * rows_f32, axis=-1, keepdims=True) + epsilon)
    rows_product = rows_f32 * scale_in * grad_normed
    gain_partial = jnp.sum(rows_product, axis=0)
    stat_partial = jnp.sum(rows_product * norm_gain, axis=-1)
    heads_small = all_sum(
        jnp.concatenate([gain_partial, stat_partial, own_taps.reshape(-1)]), "heads", heads_near
    )
    normed_parts = jnp.swapaxes(
        grad_normed.astype(bf16).reshape(row_count, head_groups, feature_share), 0, 1
    )
    grad_share = reduce_scatter(normed_parts, "heads", heads_near)
    gain_share = lax.dynamic_slice_in_dim(norm_gain, head_index * feature_share, feature_share, 0)
    norm_stat = heads_small[feature_total : feature_total + row_count]
    tokens_hat = tokens.astype(f32) * scale_in
    tokens_grad = (
        cotangent.astype(f32)
        + scale_in * (grad_share * gain_share - tokens_hat * (norm_stat / feature_total)[:, None])
    ).astype(bf16)

    pieces = [
        lax.dynamic_slice_in_dim(heads_small, head_index * feature_share, feature_share, 0),
        gate_gain_grad,
        sums[:CONV_WIDTH].reshape(-1),
        sums[CONV_WIDTH],
        heads_small[feature_total + row_count :],
        small[0, :head_share],
        small[1, :head_share],
        small[2, :head_share],
    ]
    summed = all_sum(jnp.concatenate(pieces), "shard", near)
    cuts, at = [], 0
    for piece in pieces:
        cuts.append(summed[at : at + piece.shape[0]])
        at += piece.shape[0]
    bc_taps = cuts[4].reshape(CONV_WIDTH + 1, state_width)
    offset_bc = inner_share + state_share
    return (
        mixed,
        tokens_grad,
        early_sum[:, :inner_share],
        late_sum[:, :inner_share],
        late_sum[:, inner_share:offset_bc],
        late_sum[:, offset_bc:],
        early_sum[:, inner_share:].T,
        cuts[0],
        cuts[1],
        cuts[2].reshape(CONV_WIDTH, inner_share),
        cuts[3],
        bc_taps[:CONV_WIDTH],
        bc_taps[CONV_WIDTH],
        cuts[5].astype(f32),
        cuts[6] * rate[0, :head_share],
        cuts[7],
    )


def solution(mesh):
    placed = (
        P("shard", "heads"),
        P("shard", "heads"),
        P("shard", "heads"),
        P("shard", None),
        P("shard", "heads"),
        P("heads", "shard"),
        P(),
        P("heads"),
        P(None, "heads"),
        P("heads"),
        P(),
        P(),
        P("heads"),
        P("heads"),
        P("heads"),
        P("shard", "heads"),
    )
    return jax.shard_map(
        body,
        mesh=mesh,
        in_specs=placed,
        out_specs=(
            P("shard", "heads"),
            P("shard", "heads"),
            P("shard", "heads"),
            P("shard", "heads"),
            P("shard", "heads"),
            P("shard", "heads"),
            P("heads", "shard"),
            P("heads"),
            P("heads"),
            P(None, "heads"),
            P("heads"),
            P(),
            P(),
            P("heads"),
            P("heads"),
            P("heads"),
        ),
        check_vma=False,
    )
```

```python
import functools

import jax
import jax.numpy as jnp
from jax import lax
from jax.experimental import pallas as pl
from jax.experimental.pallas import tpu as pltpu
from jax.sharding import PartitionSpec as P

CONV_WIDTH = 4
LEN = 1024
BLOCK = 256
LANES = 128

epsilon = 1e-05
highest = lax.Precision.HIGHEST
f32 = jnp.float32
bf16 = jnp.bfloat16
VMEM_LIMIT = 50 * 1024 * 1024


def dot(left, right, left_dim=1, right_dim=0, precision=None):
    return lax.dot_general(
        left,
        right,
        (((left_dim,), (right_dim,)), ((), ())),
        precision=precision,
        preferred_element_type=f32,
    )


def spreader(head_share, head_size):
    row = lax.broadcasted_iota(jnp.int32, (LANES, head_share * head_size), 0)
    head = lax.broadcasted_iota(jnp.int32, (LANES, head_share * head_size), 1) // head_size
    return (row == head).astype(bf16)


def lower_mask(size):
    row = lax.broadcasted_iota(jnp.int32, (size, size), 0)
    col = lax.broadcasted_iota(jnp.int32, (size, size), 1)
    return row >= col


def const_spec(array):
    return pl.BlockSpec(array.shape, lambda i: (0,) * array.ndim)


def scalar_spec():
    return pl.BlockSpec(memory_space=pltpu.SMEM)


def cost(micros):
    return pl.CostEstimate(flops=int(micros * 1e9), bytes_accessed=0, transcendentals=0)


def params():
    return pltpu.CompilerParams(vmem_limit_bytes=VMEM_LIMIT)


def out(shape, kind):
    return jax.ShapeDtypeStruct(shape, kind)


def row_of(index, size):
    return pl.ds(pl.multiple_of(index * size, size), size)


def silu_slope(values):
    sig = jax.nn.sigmoid(values)
    return sig * (1.0 + values * (1.0 - sig))


def row_sums(values):
    return dot(jnp.ones((8, values.shape[1]), bf16), values.astype(bf16), 1, 1)


def split(values, count):
    terms = []
    for _ in range(count):
        terms.append(values.astype(bf16))
        values = values - terms[-1].astype(f32)
    return terms


def select_rows(ones, values, count=3):
    return sum(dot(ones, term) for term in split(values, count))


def spread_lanes(values, spread, count):
    return sum(dot(term, spread) for term in split(values, count))


def decay_strips(cum, cum_t, head):
    mid = BLOCK // 2
    row = cum_t[head : head + 1, :]
    top = jnp.exp(jnp.minimum(cum[:mid, head : head + 1] - row[:, :mid], 0.0))
    low = jnp.exp(jnp.minimum(cum[mid:, head : head + 1] - row, 0.0))
    return top, low


def forward_kernel(
    sizes,
    me_ref,
    *refs,
):
    head_share, head_size, blocks_per_seq, rels, groups = sizes
    piece_refs, refs = refs[:groups], refs[groups:]
    (
        first_ref,
        second_ref,
        other_first,
        other_second,
        gain_ref,
        x_taps_ref,
        x_bias_ref,
        s_taps_ref,
        s_bias_ref,
        step_bias_ref,
        rate_ref,
        skip_ref,
        normed_ref,
        scale_ref,
        inner_ref,
        x_pre_ref,
        x_ref,
        state_in_ref,
        s_pre_ref,
        bc_ref,
        step_ref,
        cum_ref,
        start_ref,
        scanned_ref,
        weight_ref,
        x_buf,
        s_buf,
        state,
    ) = refs
    inner = head_share * head_size
    half = s_bias_ref.shape[1] // 2
    share = piece_refs[0].shape[1]

    @pl.when(pl.program_id(0) == 0)
    def _():
        own_first = me_ref[2] == 0
        for i, rel in enumerate(rels):
            rows = row_of(me_ref[0] ^ rel, first_ref.shape[1])
            held = len(rels) // 2
            part = first_ref[i] if i < held else second_ref[i - held]
            mine = part[:, inner : inner + half]
            others = other_first[i] if i < held else other_second[i - held]
            weight_ref[rows, :inner] = part[:, :inner]
            weight_ref[rows, inner : inner + half] = jnp.where(own_first, mine, others)
            weight_ref[rows, inner + half : inner + 2 * half] = jnp.where(own_first, others, mine)
            weight_ref[rows, inner + 2 * half :] = part[:, inner + half :]

    @pl.when(pl.program_id(0) % blocks_per_seq == 0)
    def _():
        x_buf[0:8, :] = jnp.zeros((8, inner), f32)
        s_buf[0:8, :] = jnp.zeros((8, 2 * half), f32)
        state[...] = jnp.zeros(state.shape, f32)

    pieces = [ref[...].astype(f32) for ref in piece_refs]
    squares = pieces[0] * pieces[0]
    for piece in pieces[1:]:
        squares = squares + piece * piece
    mean = jnp.sum(squares, axis=-1, keepdims=True) / (share * groups)
    scale = lax.rsqrt(mean + epsilon)
    scale_ref[...] = jnp.broadcast_to(scale, scale_ref.shape)
    for rel, piece in enumerate(pieces):
        at = row_of(me_ref[1] ^ rel, share)
        normed_ref[:, at] = (piece * scale * gain_ref[:, at]).astype(bf16)
    projected = dot(normed_ref[...], weight_ref[...])
    inner_in = projected[:, :inner]
    state_in = projected[:, inner : inner + 2 * half]
    step_pre = projected[:, inner + 2 * half :] + step_bias_ref[...]
    inner_ref[...] = inner_in.astype(bf16)
    state_in_ref[...] = state_in.astype(bf16)
    step_ref[...] = step_pre

    def conv(buf, values, taps_ref, bias_ref):
        buf[8 : 8 + BLOCK, :] = values
        total = bias_ref[...] + taps_ref[3:4, :] * values
        for tap in range(CONV_WIDTH - 1):
            total = total + taps_ref[tap : tap + 1, :] * buf[5 + tap : 5 + tap + BLOCK, :]
        buf[0:8, :] = buf[BLOCK : BLOCK + 8, :]
        return total

    x_pre = conv(x_buf, inner_in, x_taps_ref, x_bias_ref)
    x_pre_ref[...] = x_pre.astype(bf16)
    x = (x_pre * jax.nn.sigmoid(x_pre)).astype(bf16)
    x_ref[...] = x
    s_pre = conv(s_buf, state_in, s_taps_ref, s_bias_ref)
    s_pre_ref[...] = s_pre.astype(bf16)
    bc = (s_pre * jax.nn.sigmoid(s_pre)).astype(bf16)
    bc_ref[...] = bc
    b, c = bc[:, :half], bc[:, half:]

    steps = jax.nn.softplus(step_pre)
    lower = lower_mask(BLOCK)
    cum = select_rows(lower.astype(bf16), steps * rate_ref[...])
    cum_ref[...] = cum
    cum_t = cum.T
    spread = spreader(head_share, head_size)
    cum_x = spread_lanes(cum, spread, 3)
    steps_x = spread_lanes(steps, spread, 2)
    last = cum_x[BLOCK - 1 :, :]
    x_f32 = x.astype(f32)
    stepped = x_f32 * steps_x
    stepped_low = stepped.astype(bf16)

    old = state[...]
    old_low = old.astype(bf16)
    start_ref[0] = old_low
    base = dot(c, old_low) * jnp.exp(cum_x) + skip_ref[...] * x_f32
    weighted = (stepped * jnp.exp(last - cum_x)).astype(bf16)
    state[...] = old * jnp.exp(last) + dot(b, weighted, 0, 0)

    scores = jnp.where(lower, dot(c, b, 1, 1), 0.0)
    mid = BLOCK // 2
    top_scores, low_scores = scores[:mid, :mid], scores[mid:, :]
    pair = LANES // head_size
    lane_head = lax.broadcasted_iota(jnp.int32, (mid, LANES), 1) // head_size
    for first in range(0, head_share, pair):
        at = first * head_size
        values = stepped_low[:, at : at + LANES]
        for k in range(pair):
            top, low = decay_strips(cum, cum_t, first + k)
            top_term = dot((top * top_scores).astype(bf16), values[:mid])
            low_term = dot((low * low_scores).astype(bf16), values)
            if k == 0:
                top_total, low_total = top_term, low_term
            else:
                top_total = jnp.where(lane_head == k, top_term, top_total)
                low_total = jnp.where(lane_head == k, low_term, low_total)
        scanned_ref[:mid, at : at + LANES] = base[:mid, at : at + LANES] + top_total
        scanned_ref[mid:, at : at + LANES] = base[mid:, at : at + LANES] + low_total


def forward_scan(me, pieces, weights, consts, head_share, head_size, rels):
    count, share = pieces[0].shape
    groups = len(pieces)
    features = share * groups
    inner = head_share * head_size
    state2 = consts[3].shape[1]
    blocks = count // BLOCK
    per = lambda width: pl.BlockSpec((BLOCK, width), lambda i: (i, 0))
    outs = [
        (features, bf16),
        (LANES, f32),
        (inner, bf16),
        (inner, bf16),
        (inner, bf16),
        (state2, bf16),
        (state2, bf16),
        (state2, bf16),
        (LANES, f32),
        (LANES, f32),
    ]
    wide = inner + state2 + LANES
    return pl.pallas_call(
        functools.partial(
            forward_kernel, (head_share, head_size, LEN // BLOCK, rels, groups)
        ),
        grid=(blocks,),
        in_specs=[scalar_spec()]
        + [per(share)] * groups
        + [const_spec(a) for a in (*weights, *consts)],
        out_specs=[per(w) for w, _ in outs]
        + [
            pl.BlockSpec((1, state2 // 2, inner), lambda i: (i, 0, 0)),
            per(inner),
            pl.BlockSpec((features, wide), lambda i: (0, 0)),
        ],
        out_shape=[out((count, w), k) for w, k in outs]
        + [
            out((blocks, state2 // 2, inner), bf16),
            out((count, inner), f32),
            out((features, wide), bf16),
        ],
        scratch_shapes=[
            pltpu.VMEM((BLOCK + 8, inner), f32),
            pltpu.VMEM((BLOCK + 8, state2), f32),
            pltpu.VMEM((state2 // 2, inner), f32),
        ],
        compiler_params=params(),
        cost_estimate=cost(16),
    )(me, *pieces, *weights, *consts)


def gate_kernel(sizes, me_ref, *refs):
    z_rels, o_rels, groups = sizes
    cot_refs, refs = refs[:groups], refs[groups:]
    z_first, z_second, o_first, o_second, normed_ref, scanned_ref, gain_ref = refs[:7]
    gate_ref, grad_mid_ref, stats_ref, z_ref, o_ref = refs[7:]
    share = cot_refs[0].shape[1]

    @pl.when(pl.program_id(0) == 0)
    def _():
        held = len(z_rels) // 2
        for i in range(len(z_rels)):
            rows = row_of(me_ref[0] ^ z_rels[i], z_first.shape[1])
            z_ref[rows, :] = z_first[i] if i < held else z_second[i - held]
            rows = row_of(me_ref[0] ^ o_rels[i], z_first.shape[1])
            o_ref[rows, :] = o_first[i] if i < held else o_second[i - held]

    gate_in = dot(normed_ref[...], z_ref[...])
    grad_mid = sum(
        dot(ref[...], o_ref[row_of(me_ref[1] ^ rel, share), :])
        for rel, ref in enumerate(cot_refs)
    )
    gate_ref[...] = gate_in.astype(gate_ref.dtype)
    grad_mid_ref[...] = grad_mid.astype(grad_mid_ref.dtype)
    mixed_in = scanned_ref[...] * (gate_in * jax.nn.sigmoid(gate_in))
    squares = row_sums(mixed_in * mixed_in)
    products = row_sums(grad_mid * gain_ref[...] * mixed_in)
    row = lax.broadcasted_iota(jnp.int32, squares.shape, 0)
    stats_ref[...] = jnp.where(row == 0, squares, products)


def gate(me, cots, weights, normed, scanned, gain, z_rels, o_rels):
    count, share = cots[0].shape
    groups = len(cots)
    features = share * groups
    inner = scanned.shape[1]
    per = lambda width: pl.BlockSpec((BLOCK, width), lambda i: (i, 0))
    whole = pl.BlockSpec((features, inner), lambda i: (0, 0))
    return pl.pallas_call(
        functools.partial(gate_kernel, (z_rels, o_rels, groups)),
        grid=(count // BLOCK,),
        in_specs=[scalar_spec()]
        + [per(share)] * groups
        + [const_spec(a) for a in weights]
        + [per(features), per(inner), const_spec(gain)],
        out_specs=[
            per(inner),
            per(inner),
            pl.BlockSpec((8, BLOCK), lambda i: (0, i)),
            whole,
            whole,
        ],
        out_shape=[
            out((count, inner), f32),
            out((count, inner), bf16),
            out((8, count), f32),
            out((features, inner), bf16),
            out((features, inner), bf16),
        ],
        compiler_params=params(),
        cost_estimate=cost(8),
    )(me, *cots, *weights, normed, scanned, gain)


def mix_kernel(sizes, me_ref, *refs):
    z_rels, o_rels, groups = sizes
    cot_refs, refs = refs[:groups], refs[groups:]
    stats_ref, normed_ref, gate_ref, grad_mid_ref, scanned_ref, o_ref, gain_ref = refs[:7]
    (
        grad_scanned_ref,
        grad_gate_ref,
        out_send,
        out_keep,
        z_send,
        z_keep,
        o_send,
        o_keep,
        gain_grad_ref,
        z_sum,
        o_sum,
    ) = refs[7:]
    inner = gain_ref.shape[1]
    share = out_send.shape[2]

    @pl.when(pl.program_id(0) == 0)
    def _():
        z_sum[...] = jnp.zeros(z_sum.shape, f32)
        o_sum[...] = jnp.zeros(o_sum.shape, f32)
        gain_grad_ref[...] = jnp.zeros(gain_grad_ref.shape, f32)

    stats = stats_ref[...].T
    total = inner * groups
    scale = lax.rsqrt(stats[:, 0:1] / total + epsilon)
    mean = scale * stats[:, 1:2] / total
    gate_in = gate_ref[...]
    sig = jax.nn.sigmoid(gate_in)
    act = gate_in * sig
    scanned = scanned_ref[...]
    mid_hat = scanned * act * scale
    grad_mid = grad_mid_ref[...].astype(f32)
    normed_mid = (mid_hat * gain_ref[...]).astype(bf16)
    gain_grad_ref[0:1, :] += jnp.sum(mid_hat * grad_mid, axis=0, keepdims=True)
    grad_mixed = scale * (grad_mid * gain_ref[...] - mid_hat * mean)
    grad_scanned_ref[...] = (grad_mixed * act).astype(bf16)
    grad_gate = (grad_mixed * scanned * sig * (1.0 + gate_in * (1.0 - sig))).astype(bf16)
    grad_gate_ref[...] = grad_gate
    z_sum[...] += dot(normed_ref[...], grad_gate, 0, 0)
    for rel in range(groups):
        rows = row_of(me_ref[1] ^ rel, share)
        o_sum[rows, :] += dot(cot_refs[rel][...], normed_mid, 0, 0)
        part = dot(normed_mid, o_ref[rows, :], 1, 1).astype(bf16)
        if rel % 2:
            out_send[rel // 2] = part
        else:
            out_keep[rel // 2] = part

    @pl.when(pl.program_id(0) == pl.num_programs(0) - 1)
    def _():
        size = z_send.shape[1]
        for refs_of, total, rels in ((z_send, z_sum, z_rels[0]), (z_keep, z_sum, z_rels[1]), (o_send, o_sum, o_rels[0]), (o_keep, o_sum, o_rels[1])):
            for i, rel in enumerate(rels):
                refs_of[i] = total[row_of(me_ref[0] ^ rel, size), :].astype(bf16)


def mix(me, cots, stats, normed, gate_in, grad_mid, scanned, o_weight, gain, shards, z_rels, o_rels):
    groups = len(cots)
    count, inner = scanned.shape
    features = normed.shape[1]
    share = features // groups
    size = features // shards
    per = lambda width: pl.BlockSpec((BLOCK, width), lambda i: (i, 0))
    parts = pl.BlockSpec((groups // 2, BLOCK, share), lambda i: (0, i, 0))
    early = (shards // 2, size, inner)
    fixed = pl.BlockSpec(early, lambda i: (0, 0, 0))
    return pl.pallas_call(
        functools.partial(mix_kernel, (z_rels, o_rels, groups)),
        grid=(count // BLOCK,),
        in_specs=[scalar_spec()]
        + [per(share)] * groups
        + [
            pl.BlockSpec((8, BLOCK), lambda i: (0, i)),
            per(features),
            per(inner),
            per(inner),
            per(inner),
            const_spec(o_weight),
            const_spec(gain),
        ],
        out_specs=[
            per(inner),
            per(inner),
            parts,
            parts,
            fixed,
            fixed,
            fixed,
            fixed,
            pl.BlockSpec((8, inner), lambda i: (0, 0)),
        ],
        out_shape=[
            out((count, inner), bf16),
            out((count, inner), bf16),
            out((groups // 2, count, share), bf16),
            out((groups // 2, count, share), bf16),
            out(early, bf16),
            out(early, bf16),
            out(early, bf16),
            out(early, bf16),
            out((8, inner), f32),
        ],
        scratch_shapes=[pltpu.VMEM((features, inner), f32)] * 2,
        compiler_params=params(),
        cost_estimate=cost(10),
    )(me, *cots, stats, normed, gate_in, grad_mid, scanned, o_weight, gain)


def backward_kernel(sizes, *refs):
    me_ref = refs[0]
    head_share, head_size, blocks_per_seq, top_block, joined = sizes
    inputs, upper_parts, refs = refs[1:21], refs[21] if joined else None, refs[21 + joined :]
    (
        grad_ref,
        inner_ref,
        x_pre_ref,
        x_ref,
        state_in_ref,
        s_pre_ref,
        bc_ref,
        step_ref,
        cum_ref,
        start_ref,
        x_taps_ref,
        s_taps_ref,
        rate_ref,
        skip_ref,
    ) = inputs[:14]
    given = inputs[14:]
    late_ref, s_parts, *carried_refs = refs
    x_sums, s_sums, small_ref, x_tail, s_tail, state, x_buf, s_buf = carried_refs
    inner = head_share * head_size
    half = bc_ref.shape[1] // 2
    at_block = top_block - pl.program_id(0)

    @pl.when(pl.program_id(0) == 0)
    def _():
        for ref, value in zip((x_sums, s_sums, small_ref, x_tail, s_tail, state), given):
            ref[...] = value[...]

    @pl.when(at_block % blocks_per_seq == blocks_per_seq - 1)
    def _():
        x_tail[...] = jnp.zeros(x_tail.shape, f32)
        s_tail[...] = jnp.zeros(s_tail.shape, f32)
        state[...] = jnp.zeros(state.shape, f32)

    grad_low = grad_ref[...]
    grad = grad_low.astype(f32)
    x = x_ref[...].astype(f32)
    bc = bc_ref[...]
    b, c = bc[:, :half], bc[:, half:]
    step_pre = step_ref[...]
    steps = jax.nn.softplus(step_pre)
    cum = cum_ref[...]
    cum_t = cum.T
    lower = lower_mask(BLOCK)
    row = lax.broadcasted_iota(jnp.int32, (BLOCK, BLOCK), 0)
    col = lax.broadcasted_iota(jnp.int32, (BLOCK, BLOCK), 1)
    spread = spreader(head_share, head_size)
    cum_x = spread_lanes(cum, spread, 3)
    steps_x = spread_lanes(steps, spread, 2)
    last = cum_x[BLOCK - 1 :, :]
    decay_in = jnp.exp(cum_x)
    decay_out = jnp.exp(last - cum_x)
    stepped = x * steps_x
    stepped_low = stepped.astype(bf16)

    old_low = start_ref[0]
    old = old_low.astype(f32)
    later = state[...]
    later_low = later.astype(bf16)
    grad_decayed = grad * decay_in
    grad_decayed_low = grad_decayed.astype(bf16)
    from_later = dot(b, later_low) * decay_out
    carried = dot(c, old_low)
    grad_c = dot(grad_decayed_low, old_low, 1, 1)
    grad_b = dot((stepped * decay_out).astype(bf16), later_low, 1, 1)
    state[...] = later * jnp.exp(last) + dot(c, grad_decayed_low, 0, 0)

    scores = jnp.where(lower, dot(c, b, 1, 1), 0.0)
    mid = BLOCK // 2
    top_scores, low_scores = scores[:mid, :mid], scores[mid:, :]
    pair = LANES // head_size
    lane_head = lax.broadcasted_iota(jnp.int32, (BLOCK, LANES), 1) // head_size
    pick_lane = lax.broadcasted_iota(jnp.int32, (BLOCK, LANES), 1)
    top_sum = jnp.zeros((mid, mid), f32)
    low_sum = jnp.zeros((mid, BLOCK), f32)
    top_cross = jnp.zeros((mid, LANES), f32)
    low_cross = jnp.zeros((mid, LANES), f32)
    all_cross = jnp.zeros((BLOCK, LANES), f32)
    within = []
    for first in range(0, head_share, pair):
        at = first * head_size
        grads = grad_low[:, at : at + LANES]
        values = stepped_low[:, at : at + LANES]
        total = None
        for k in range(pair):
            top, low = decay_strips(cum, cum_t, first + k)
            own = jnp.where(lane_head == k, grads, jnp.zeros_like(grads))
            pick = (pick_lane == first + k).astype(bf16)
            top_products = dot(own[:mid], values[:mid], 1, 1) * top
            low_products = dot(own[mid:], values, 1, 1) * low
            top_sum = top_sum + top_products
            low_sum = low_sum + low_products
            low_term = dot((low * low_scores).astype(bf16), grads[mid:], 0, 0)
            top_term = dot((top * top_scores).astype(bf16), grads[:mid], 0, 0)
            term = low_term + jnp.concatenate([top_term, jnp.zeros_like(top_term)], axis=0)
            total = term if k == 0 else jnp.where(lane_head == k, term, total)
            top_pairs = (top_products * top_scores).astype(bf16)
            low_pairs = (low_products * low_scores).astype(bf16)
            top_cross = top_cross + dot(top_pairs, pick[:mid]) - dot(top_pairs, pick[:mid], 0, 0)
            low_cross = low_cross + dot(low_pairs, pick)
            all_cross = all_cross + dot(low_pairs, pick[mid:], 0, 0)
        within.append(total)
    zeros = jnp.zeros((mid, mid), f32)
    gathered = jnp.concatenate([jnp.concatenate([top_sum, zeros], axis=1), low_sum], axis=0)
    gathered_low = jnp.where(lower, gathered, 0.0).astype(bf16)
    grad_b = grad_b + dot(gathered_low, c, 0, 0)
    grad_c = grad_c + dot(gathered_low, b)
    crossing = jnp.concatenate([top_cross, low_cross], axis=0) - all_cross

    by_x = jnp.concatenate(within, axis=1) + from_later
    fold = lambda values: dot(values.astype(bf16), spread, 1, 1)
    direct = fold(by_x * x)
    into = fold(grad_decayed * carried)
    onward = steps * fold(from_later * x)
    tops = jnp.sum(later * old, axis=0, keepdims=True) * jnp.exp(last)
    spanning = fold(jnp.broadcast_to(tops, (8, inner)))[0:1, :]
    upper = (row <= col).astype(bf16)
    strict = (row > col).astype(bf16)
    by_decay = select_rows(upper, into + crossing, 3) + select_rows(strict, onward, 2) + spanning
    by_step = direct + rate_ref[...] * by_decay
    grad_step = by_step * jax.nn.sigmoid(step_pre)
    small_ref[0:1, :] += jnp.sum(grad_step, axis=0, keepdims=True)
    small_ref[1:2, :] += jnp.sum(steps * by_decay, axis=0, keepdims=True)
    skips = jnp.sum(grad * x, axis=0, keepdims=True)
    small_ref[2:3, :] += sum(
        dot(term, spread, 1, 1) for term in split(jnp.broadcast_to(skips, (8, inner)), 2)
    )[0:1, :]

    def conv_back(buf, tail, by_pre, values, taps_ref, sums):
        buf[0:BLOCK, :] = by_pre
        buf[BLOCK:, :] = tail[...]
        tail[...] = by_pre[0:8, :]
        total = taps_ref[3:4, :] * by_pre
        sums[3:4, :] += jnp.sum(by_pre * values, axis=0, keepdims=True)
        sums[4:5, :] += jnp.sum(by_pre, axis=0, keepdims=True)
        for tap in range(CONV_WIDTH - 1):
            ahead = CONV_WIDTH - 1 - tap
            moved = buf[ahead : ahead + BLOCK, :]
            total = total + taps_ref[tap : tap + 1, :] * moved
            sums[tap : tap + 1, :] += jnp.sum(moved * values, axis=0, keepdims=True)
        return total.astype(bf16)

    by_conv = steps_x * by_x + skip_ref[...] * grad
    by_pre = by_conv * silu_slope(x_pre_ref[...].astype(f32))
    late_ref[:, :inner] = conv_back(
        x_buf, x_tail, by_pre, inner_ref[...].astype(f32), x_taps_ref, x_sums
    )
    by_state = jnp.concatenate([grad_b, grad_c], axis=1) * silu_slope(s_pre_ref[...].astype(f32))
    grad_state = conv_back(
        s_buf, s_tail, by_state, state_in_ref[...].astype(f32), s_taps_ref, s_sums
    )
    late_ref[:, inner : inner + 2 * half] = grad_state
    width = half // 2
    first = lax.broadcasted_iota(jnp.int32, (BLOCK, half), 1) < width
    left, right = grad_state[:, :half], grad_state[:, half:]
    turn = lambda v: jnp.concatenate([v[:, width:], v[:, :width]], axis=1)
    even, odd = jnp.where(first, left, turn(right)), jnp.where(first, turn(left), right)
    own_first, low_side = me_ref[2] == 0, me_ref[1] < 2
    for core, (one, other) in enumerate(((even, odd), (odd, even))):
        half_of = jnp.where(own_first, one, other)
        turned = turn(half_of)
        for side, part in enumerate((jnp.where(low_side, half_of, turned), jnp.where(low_side, turned, half_of))):
            if joined:
                part = jnp.where(first, part, turn(upper_parts[core + 2 * side]))
            s_parts[core + 2 * side] = part
    late_ref[:, inner + 2 * half :] = grad_step.astype(bf16)


def backward_scan(me, part, rows, starts, consts, carry, upper, head_share, head_size):
    first, stop = part
    count, inner = rows[0].shape
    state2 = rows[6].shape[1]
    wide = inner + state2 + LANES
    per = lambda width: pl.BlockSpec((BLOCK, width), lambda i: (stop - 1 - i, 0))
    joined = [] if upper is None else list(upper)[::-1]
    sizes = (head_share, head_size, LEN // BLOCK, stop - 1, len(joined))
    state_parts = pl.BlockSpec((4, BLOCK, state2 // 2), lambda i: (0, stop - first - 1 - i, 0))
    results = pl.pallas_call(
        functools.partial(backward_kernel, sizes),
        grid=(stop - first,),
        in_specs=[scalar_spec()]
        + [per(a.shape[1]) for a in rows]
        + [pl.BlockSpec((1, state2 // 2, inner), lambda i: (stop - 1 - i, 0, 0))]
        + [const_spec(a) for a in (*consts, *carry)]
        + ([state_parts, pl.BlockSpec(memory_space=pl.ANY)] if joined else []),
        out_specs=[per(wide)]
        + [state_parts]
        + [const_spec(a) for a in carry],
        out_shape=[out((count, wide), bf16)]
        + [out((4, (stop - first) * BLOCK, state2 // 2), bf16)]
        + [out(a.shape, f32) for a in carry],
        input_output_aliases={len(rows) + 3 + len(consts) + len(carry): 0} if joined else {},
        scratch_shapes=[
            pltpu.VMEM((BLOCK + 8, inner), f32),
            pltpu.VMEM((BLOCK + 8, state2), f32),
        ],
        compiler_params=params(),
        cost_estimate=cost(12),
    )(me, *rows, starts, *consts, *carry, *joined)
    return results[0], results[1], tuple(results[2:])


def late_kernel(sizes, me_ref, *refs):
    a_rels, b_rels, inner, half = sizes
    late_ref, state_ref, normed_ref, a_send, a_keep, b_send, b_keep, total = refs

    @pl.when(pl.program_id(0) == 0)
    def _():
        total[...] = jnp.zeros(total.shape, f32)

    rest = inner + 2 * half
    width = LANES // 2
    turn = lambda v: jnp.concatenate([v[:, width:], v[:, :width]], axis=1)
    steps = turn(late_ref[:, rest:])
    state = state_ref[...]
    state = jnp.where(pl.program_id(0) < pl.num_programs(0) // 2, state, turn(state))
    first = lax.broadcasted_iota(jnp.int32, (BLOCK, LANES), 1) < width
    both = jnp.concatenate([late_ref[:, :inner], jnp.where(first, state, steps)], axis=1)
    total[...] += dot(normed_ref[...], both, 0, 0)

    @pl.when(pl.program_id(0) == pl.num_programs(0) - 1)
    def _():
        size, cut = a_send.shape[1:]
        for rels, send, keep, columns in (
            (a_rels, a_send, a_keep, slice(0, cut)),
            (b_rels, b_send, b_keep, slice(cut, None)),
        ):
            for to, found in zip((send, keep), rels):
                for i, rel in enumerate(found):
                    to[i] = total[row_of(me_ref[0] ^ rel, size), columns].astype(bf16)


def late_grads(me, late, state, normed, inner, half, shards, a_rels, b_rels):
    count, wide = late.shape
    features = normed.shape[1]
    size = features // shards
    cut = inner // 2
    per = lambda width: pl.BlockSpec((BLOCK, width), lambda i: (i, 0))
    packed = pl.BlockSpec((BLOCK, LANES), lambda i: (i % (count // BLOCK // 2), 0))
    a_part, b_part = (shards // 2, size, cut), (shards // 2, size, inner + LANES - cut)
    outs = [a_part, a_part, b_part, b_part]
    return pl.pallas_call(
        functools.partial(late_kernel, (a_rels, b_rels, inner, half)),
        grid=(count // BLOCK,),
        in_specs=[scalar_spec(), per(wide), packed, per(features)],
        out_specs=[pl.BlockSpec(dims, lambda i: (0, 0, 0)) for dims in outs],
        out_shape=[out(dims, bf16) for dims in outs],
        scratch_shapes=[pltpu.VMEM((features, inner + LANES), f32)],
        compiler_params=params(),
        cost_estimate=cost(5),
    )(me, late, state, normed)


def rows_kernel(groups, me_ref, *refs):
    piece_refs, refs = refs[:groups], refs[groups:]
    late_ref, gate_grad_ref, scale_ref, z_ref, weight_ref, gain_ref = refs[:6]
    rows_send, rows_keep, gain_grad_ref, stat_ref = refs[6:]
    share = piece_refs[0].shape[1]

    @pl.when(pl.program_id(0) == 0)
    def _():
        gain_grad_ref[...] = jnp.zeros(gain_grad_ref.shape, f32)

    grad_gate = gate_grad_ref[...]
    late = late_ref[...]
    scale = scale_ref[:, 0:1]
    stat = jnp.zeros((BLOCK, share), f32)
    for rel in range(groups):
        rows = row_of(me_ref[0 + 1] ^ rel, share)
        part = dot(grad_gate, z_ref[rows, :], 1, 1) + dot(late, weight_ref[rows, :], 1, 1)
        to = rows_send if rel % 2 else rows_keep
        to[rel // 2] = part.astype(bf16)
        product = piece_refs[rel][...].astype(f32) * scale * part
        gain_grad_ref[0:1, rows] += jnp.sum(product, axis=0, keepdims=True)
        stat = stat + product * gain_ref[:, rows]
    stat_ref[...] = row_sums(stat)


def row_grads(me, pieces, late, grad_gate, scale, z_all, weight, gain):
    count, share = pieces[0].shape
    groups = len(pieces)
    features = share * groups
    per = lambda width: pl.BlockSpec((BLOCK, width), lambda i: (i, 0))
    parts = pl.BlockSpec((groups // 2, BLOCK, share), lambda i: (0, i, 0))
    return pl.pallas_call(
        functools.partial(rows_kernel, groups),
        grid=(count // BLOCK,),
        in_specs=[scalar_spec()]
        + [per(a.shape[1]) for a in (*pieces, late, grad_gate, scale)]
        + [const_spec(a) for a in (z_all, weight, gain)],
        out_specs=[
            parts,
            parts,
            pl.BlockSpec((8, features), lambda i: (0, 0)),
            pl.BlockSpec((8, BLOCK), lambda i: (0, i)),
        ],
        out_shape=[
            out((groups // 2, count, share), bf16),
            out((groups // 2, count, share), bf16),
            out((8, features), f32),
            out((8, count), f32),
        ],
        compiler_params=params(),
        cost_estimate=cost(6),
    )(me, *pieces, late, grad_gate, scale, z_all, weight, gain)


def swap(value, axis, step):
    count = lax.axis_size(axis)
    return lax.ppermute(value, axis, [(i, i ^ step) for i in range(count)])


def steps_of(axis):
    found = []
    while 2 ** len(found) < lax.axis_size(axis):
        found.append(2 ** len(found))
    return found


def rels_of(order):
    rels = [0]
    for step in order:
        rels = rels + [rel ^ step for rel in rels]
    return rels


def halves_of(order):
    rels = rels_of(order[:0:-1])
    return [rel ^ order[0] for rel in rels], rels


def gather_steps(value, axis, order):
    held = value[None]
    for i, step in enumerate(order):
        held, got = yield held, swap(held, axis, step)
        if i < len(order) - 1:
            held = jnp.concatenate([held, got], axis=0)


def reduce_steps(send, keep, axis, order):
    for i, step in enumerate(order):
        keep, got = yield keep, swap(send, axis, step)
        if i < len(order) - 1:
            total = keep.astype(f32) + got.astype(f32)
            mid = total.shape[0] // 2
            keep, send = total[:mid], total[mid:].astype(bf16)


def pair_steps(send, keep, axis, order):
    keep, got = yield keep, swap(send, axis, order[0])
    send = (keep[1:].astype(f32) + got[1:].astype(f32)).astype(bf16)
    yield (keep, got), swap(send, axis, order[1])


def sum_steps(value, axis, order):
    for step in order:
        value, got = yield value, swap(value, axis, step)
        value = value + got


class Exchange:
    def __init__(self, steps, left=0):
        self.steps, self.value, self.ended, self.left = steps, None, False, left

    def advance(self):
        self.left -= 1
        try:
            self.value = self.steps.send(self.value)
        except StopIteration:
            self.ended = True

    def total(self):
        keep, got = self.value
        return keep.astype(f32) + got.astype(f32)


def phase(exchanges, beside=()):
    values, beside = lax.optimization_barrier(([e.value for e in exchanges], beside))
    for exchange, value in zip(exchanges, values):
        exchange.value = value
    return beside


def finish(exchanges, jobs):
    moving, results = exchanges, [None] * len(jobs)
    while moving:
        for exchange in moving:
            exchange.advance()
        moving = [exchange for exchange in moving if not exchange.ended]
        new = [i for i, job in enumerate(jobs) if job[0].ended and results[i] is None]
        made = [jobs[i][1]() for i in new]
        if any(exchange.left > 0 for exchange in moving):
            made = phase(moving, made)
        for i, result in zip(new, made):
            results[i] = result
    return results


def body(
    tokens,
    z_weight,
    x_weight,
    bc_weight,
    dt_weight,
    out_weight,
    norm_gain,
    gate_gain,
    x_conv_weight,
    x_conv_bias,
    bc_conv_weight,
    bc_conv_bias,
    step_bias,
    decay_log,
    skip_gain,
    cotangent,
):
    head_index = lax.axis_index("heads")
    shard_index = lax.axis_index("shard")
    groups = lax.axis_size("heads")
    shards = lax.axis_size("shard")
    row_count, feature_share = tokens.shape
    feature_total = feature_share * groups
    size, inner_share = z_weight.shape
    head_share = dt_weight.shape[1]
    head_size = inner_share // head_share
    state_width = bc_weight.shape[1]
    half = state_width // 2
    near = steps_of("shard")
    far = near[::-1]
    rels = rels_of(far)
    core = head_index % 2
    me = jnp.stack([shard_index, head_index, core]).astype(jnp.int32)
    step_pad = LANES - head_share

    own_half = lax.dynamic_slice_in_dim(bc_weight, core * half, half, 1)
    scan_weight = jnp.concatenate(
        [x_weight, own_half, jnp.pad(dt_weight, ((0, 0), (0, step_pad)))], axis=1
    )
    o_order = near[:1] + far[:-1]
    scan_x = Exchange(gather_steps(scan_weight, "shard", far))
    z_x = Exchange(gather_steps(z_weight, "shard", far))
    o_x = Exchange(gather_steps(out_weight.T, "shard", o_order), len(far))
    last = len(far) - 1
    cut = lambda v: v[:, :, inner_share : inner_share + half]
    for i in range(len(far)):
        scan_x.advance()
        moving = [scan_x]
        if i > 0:
            z_x.advance()
            moving.append(z_x)
        if i != 1:
            o_x.advance()
            moving.append(o_x)
        if i == 0:
            beside = (swap(tokens, "heads", 2), swap(tokens, "heads", 1))
            tokens_across, tokens_near, z_from, cot_from = phase(
                moving, (*beside, z_weight, cotangent)
            )
            z_x = Exchange(gather_steps(z_from, "shard", far), len(far))
        elif i == last:
            beside = (
                swap(tokens_across, "heads", 1),
                swap(cot_from, "heads", 2),
                swap(cut(scan_x.value[0]), "heads", 1),
            )
            tokens_last, cot_across, other_held = phase(moving, beside)
        else:
            (cot_from,) = phase(moving, (cot_from,))
    scan_held, scan_got = scan_x.value
    token_parts = [tokens, tokens_near, tokens_across, tokens_last]
    other_got = swap(cut(scan_got), "heads", 1)

    pad_lanes = lambda v: jnp.pad(v, (0, step_pad))[None]
    rate = pad_lanes(-jnp.exp(decay_log))
    skip_x = jnp.repeat(skip_gain, head_size)[None]
    z_x.advance()
    o_x.advance()
    cot_near, cot_last = swap(cot_from, "heads", 1), swap(cot_across, "heads", 1)
    scan = forward_scan(
        me,
        token_parts,
        (scan_held, scan_got, other_held, other_got),
        (
            norm_gain[None],
            x_conv_weight,
            x_conv_bias[None],
            bc_conv_weight,
            bc_conv_bias[None],
            pad_lanes(step_bias),
            rate,
            skip_x,
        ),
        head_share,
        head_size,
        rels,
    )

    (
        normed,
        scale_in,
        inner_in,
        x_pre,
        x,
        state_in,
        s_pre,
        bc,
        step_pre,
        cum,
        starts,
        scanned,
        scan_weight_all,
    ), (cot_near, cot_last) = phase([z_x, o_x], (scan, (cot_near, cot_last)))
    finish([z_x, o_x], [])
    cot_parts = [cotangent, cot_near, cot_across, cot_last]

    gain_row = gate_gain[None]
    gate_in, grad_mid, stats, z_all, o_all = gate(
        me, cot_parts, (*z_x.value, *o_x.value), normed, scanned, gain_row, rels, rels_of(o_order)
    )
    for step in (1, 2):
        stats = stats + swap(stats, "heads", step)

    send_rels, keep_rels = halves_of(near)
    o_sums = near[1:] + near[:1]
    (
        grad_scanned,
        grad_gate,
        out_send,
        out_keep,
        z_send,
        z_keep,
        o_send,
        o_keep,
        gate_gain_grad,
    ) = mix(
        me, cot_parts, stats, normed, gate_in, grad_mid, scanned, o_all, gain_row,
        shards, (send_rels, keep_rels), halves_of(o_sums),
    )
    z_x = Exchange(reduce_steps(z_send, z_keep, "shard", near), len(near))
    o_x = Exchange(reduce_steps(o_send, o_keep, "shard", o_sums), len(near))
    out_x = Exchange(reduce_steps(out_send, out_keep, "heads", [1, 2]))

    blocks = row_count // BLOCK
    carry = tuple(
        jnp.zeros(dims, f32)
        for dims in (
            (8, inner_share),
            (8, state_width),
            (8, LANES),
            (8, inner_share),
            (8, state_width),
            (half, inner_share),
        )
    )
    scan_rows = (grad_scanned, inner_in, x_pre, x, state_in, s_pre, bc, step_pre, cum)
    scan_consts = (x_conv_weight, bc_conv_weight, rate, skip_x)
    sizes = (head_share, head_size)
    quarter = half // 2
    for exchange in (z_x, o_x, out_x):
        exchange.advance()
    late, s_upper, carry = phase(
        [z_x, o_x, out_x],
        backward_scan(me, (blocks // 2, blocks), scan_rows, starts, scan_consts, carry, None, *sizes),
    )
    for exchange in (z_x, o_x, out_x):
        exchange.advance()
    late, state_parts, carry = phase(
        [z_x, o_x, out_x],
        backward_scan(
            me, (0, blocks // 2), scan_rows, starts, scan_consts, carry, (late, s_upper), *sizes
        ),
    )
    x_sums, s_sums, small = carry[:3]
    (rows_send, rows_keep, gain_grad, stat), state_got = phase(
        [],
        (
            row_grads(
                me, token_parts, late, grad_gate, scale_in, z_all, scan_weight_all, norm_gain[None]
            ),
            [swap(state_parts[step], "heads", step) for step in (1, 2, 3)],
        ),
    )

    state_total = sum((part.astype(f32) for part in state_got), state_parts[0].astype(f32)).astype(bf16)
    b_sums = near[1:] + near[:1]
    rows_x = Exchange(pair_steps(rows_send, rows_keep, "heads", [1, 2]))
    by_heads = jnp.concatenate([gain_grad[0], stat[0], s_sums[: CONV_WIDTH + 1].reshape(-1)])
    rows_x.advance()
    (a_send, a_keep, b_send, b_keep), by_heads, got = phase(
        [rows_x, z_x, o_x],
        (
            late_grads(
                me, late, state_total, normed, inner_share, half, shards, halves_of(near), halves_of(b_sums)
            ),
            by_heads,
            [swap(by_heads, "heads", step) for step in (1, 2, 3)],
        ),
    )
    a_x = Exchange(reduce_steps(a_send, a_keep, "shard", near), len(near))
    b_x = Exchange(reduce_steps(b_send, b_keep, "shard", b_sums), len(near))
    by_heads = (by_heads + got[0]) + (got[1] + got[2])
    local = jnp.concatenate(
        [
            gate_gain_grad[0],
            x_sums[: CONV_WIDTH + 1].reshape(-1),
            small[0, :head_share],
            small[1, :head_share],
            small[2, :head_share],
        ]
    )
    summed = jnp.concatenate(
        [
            lax.dynamic_slice_in_dim(by_heads, head_index * feature_share, feature_share, 0),
            by_heads[feature_total + row_count :],
            local,
        ]
    )
    small_x = Exchange(sum_steps(summed, "shard", near), len(near))
    for exchange in (a_x, b_x, rows_x, small_x, z_x):
        exchange.advance()
    mixed = (tokens.astype(f32) + out_x.total()[0]).astype(bf16)
    norm_stat = by_heads[feature_total : feature_total + row_count]
    mixed, norm_stat = phase([a_x, b_x, rows_x, small_x, z_x], (mixed, norm_stat))
    scale = scale_in[:, :1]
    gain_share = lax.dynamic_slice_in_dim(norm_gain, head_index * feature_share, feature_share, 0)

    def token_grads():
        tokens_hat = tokens.astype(f32) * scale
        (first, second), third = rows_x.value
        total = first[0].astype(f32) + second[0].astype(f32) + third[0].astype(f32)
        scaled = total * gain_share - tokens_hat * (norm_stat / feature_total)[:, None]
        return (cotangent.astype(f32) + scale * scaled).astype(bf16)

    tokens_grad, z_sum, o_sum, a_sum, b_sum, summed = finish(
        [o_x, a_x, b_x, rows_x, small_x, z_x],
        [
            (rows_x, token_grads),
            (z_x, lambda: z_x.total()[0]),
            (o_x, lambda: o_x.total()[0].T),
            (a_x, lambda: a_x.total()[0]),
            (b_x, lambda: b_x.total()[0]),
            (small_x, small_x.total),
        ],
    )
    steps_at = inner_share - a_sum.shape[1]

    cuts, at = [], 0
    taps = CONV_WIDTH + 1
    for count in (feature_share, taps * state_width, inner_share, taps * inner_share) + (head_share,) * 3:
        cuts.append(summed[at : at + count])
        at += count
    bc_taps = cuts[1].reshape(taps, state_width)
    x_taps = cuts[3].reshape(taps, inner_share)
    return (
        mixed,
        tokens_grad,
        z_sum,
        jnp.concatenate([a_sum, b_sum[:, :steps_at]], axis=1),
        b_sum[:, steps_at : steps_at + quarter],
        b_sum[:, steps_at + LANES // 2 : steps_at + LANES // 2 + head_share],
        o_sum,
        cuts[0],
        cuts[2],
        x_taps[:CONV_WIDTH],
        x_taps[CONV_WIDTH],
        bc_taps[:CONV_WIDTH],
        bc_taps[CONV_WIDTH],
        cuts[4],
        cuts[5] * rate[0, :head_share],
        cuts[6],
    )


def solution(mesh):
    placed = (
        P("shard", "heads"),
        P("shard", "heads"),
        P("shard", "heads"),
        P("shard", None),
        P("shard", "heads"),
        P("heads", "shard"),
        P(),
        P("heads"),
        P(None, "heads"),
        P("heads"),
        P(),
        P(),
        P("heads"),
        P("heads"),
        P("heads"),
        P("shard", "heads"),
    )
    return jax.shard_map(
        body,
        mesh=mesh,
        in_specs=placed,
        out_specs=(
            P("shard", "heads"),
            P("shard", "heads"),
            P("shard", "heads"),
            P("shard", "heads"),
            P("shard", "heads"),
            P("shard", "heads"),
            P("heads", "shard"),
            P("heads"),
            P("heads"),
            P(None, "heads"),
            P("heads"),
            P(),
            P(),
            P("heads"),
            P("heads"),
            P("heads"),
        ),
        check_vma=False,
    )
```

```python
import functools

import jax
import jax.numpy as jnp
from jax import lax
from jax.experimental import pallas as pl
from jax.experimental.pallas import tpu as pltpu
from jax.sharding import PartitionSpec as P

CONV_WIDTH = 4
LEN = 1024
BLOCK = 256
LANES = 128

epsilon = 1e-05
highest = lax.Precision.HIGHEST
f32 = jnp.float32
bf16 = jnp.bfloat16
VMEM_LIMIT = 53 * 1024 * 1024


def dot(left, right, left_dim=1, right_dim=0, precision=None):
    return lax.dot_general(
        left,
        right,
        (((left_dim,), (right_dim,)), ((), ())),
        precision=precision,
        preferred_element_type=f32,
    )


def spreader(head_share, head_size):
    row = lax.broadcasted_iota(jnp.int32, (LANES, head_share * head_size), 0)
    head = lax.broadcasted_iota(jnp.int32, (LANES, head_share * head_size), 1) // head_size
    return (row == head).astype(bf16)


def lower_mask(size):
    row = lax.broadcasted_iota(jnp.int32, (size, size), 0)
    col = lax.broadcasted_iota(jnp.int32, (size, size), 1)
    return row >= col


def const_spec(array):
    return pl.BlockSpec(array.shape, lambda i: (0,) * array.ndim)


def scalar_spec():
    return pl.BlockSpec(memory_space=pltpu.SMEM)


def cost(micros):
    return pl.CostEstimate(flops=int(micros * 1e9), bytes_accessed=0, transcendentals=0)


def params():
    return pltpu.CompilerParams(vmem_limit_bytes=VMEM_LIMIT)


def out(shape, kind):
    return jax.ShapeDtypeStruct(shape, kind)


def row_of(index, size):
    return pl.ds(pl.multiple_of(index * size, size), size)


def silu_slope(values):
    sig = jax.nn.sigmoid(values)
    return sig * (1.0 + values * (1.0 - sig))


def row_sums(values):
    return dot(jnp.ones((8, values.shape[1]), bf16), values.astype(bf16), 1, 1)


def split(values, count):
    terms = []
    for _ in range(count):
        terms.append(values.astype(bf16))
        values = values - terms[-1].astype(f32)
    return terms


def select_rows(ones, values, count=3):
    return sum(dot(ones, term) for term in split(values, count))


def spread_lanes(values, spread, count):
    return sum(dot(term, spread) for term in split(values, count))


def decay_strips(cum, cum_t, head):
    mid = BLOCK // 2
    row = cum_t[head : head + 1, :]
    top = jnp.exp(jnp.minimum(cum[:mid, head : head + 1] - row[:, :mid], 0.0))
    low = jnp.exp(jnp.minimum(cum[mid:, head : head + 1] - row, 0.0))
    return top, low


def forward_kernel(
    sizes,
    me_ref,
    *refs,
):
    head_share, head_size, blocks_per_seq, rels, groups = sizes
    piece_refs, refs = refs[:groups], refs[groups:]
    (
        first_ref,
        second_ref,
        other_first,
        other_second,
        gain_ref,
        x_taps_ref,
        x_bias_ref,
        s_taps_ref,
        s_bias_ref,
        step_bias_ref,
        rate_ref,
        skip_ref,
        normed_ref,
        scale_ref,
        inner_ref,
        x_pre_ref,
        x_ref,
        state_in_ref,
        s_pre_ref,
        bc_ref,
        step_ref,
        cum_ref,
        start_ref,
        scanned_ref,
        weight_ref,
        x_buf,
        s_buf,
        state,
    ) = refs
    inner = head_share * head_size
    half = s_bias_ref.shape[1] // 2
    share = piece_refs[0].shape[1]

    @pl.when(pl.program_id(0) == 0)
    def _():
        own_first = me_ref[2] == 0
        for i, rel in enumerate(rels):
            rows = row_of(me_ref[0] ^ rel, first_ref.shape[1])
            held = len(rels) // 2
            part = first_ref[i] if i < held else second_ref[i - held]
            mine = part[:, inner : inner + half]
            others = other_first[i] if i < held else other_second[i - held]
            weight_ref[rows, :inner] = part[:, :inner]
            weight_ref[rows, inner : inner + half] = jnp.where(own_first, mine, others)
            weight_ref[rows, inner + half : inner + 2 * half] = jnp.where(own_first, others, mine)
            weight_ref[rows, inner + 2 * half :] = part[:, inner + half :]

    @pl.when(pl.program_id(0) % blocks_per_seq == 0)
    def _():
        x_buf[0:8, :] = jnp.zeros((8, inner), f32)
        s_buf[0:8, :] = jnp.zeros((8, 2 * half), f32)
        state[...] = jnp.zeros(state.shape, f32)

    pieces = [ref[...].astype(f32) for ref in piece_refs]
    squares = pieces[0] * pieces[0]
    for piece in pieces[1:]:
        squares = squares + piece * piece
    mean = jnp.sum(squares, axis=-1, keepdims=True) / (share * groups)
    scale = lax.rsqrt(mean + epsilon)
    scale_ref[...] = jnp.broadcast_to(scale, scale_ref.shape)
    for rel, piece in enumerate(pieces):
        at = row_of(me_ref[1] ^ rel, share)
        normed_ref[:, at] = (piece * scale * gain_ref[:, at]).astype(bf16)
    projected = dot(normed_ref[...], weight_ref[...])
    inner_in = projected[:, :inner]
    state_in = projected[:, inner : inner + 2 * half]
    step_pre = projected[:, inner + 2 * half :] + step_bias_ref[...]
    inner_ref[...] = inner_in.astype(bf16)
    state_in_ref[...] = state_in.astype(bf16)
    step_ref[...] = step_pre

    def conv(buf, values, taps_ref, bias_ref):
        buf[8 : 8 + BLOCK, :] = values
        total = bias_ref[...] + taps_ref[3:4, :] * values
        for tap in range(CONV_WIDTH - 1):
            total = total + taps_ref[tap : tap + 1, :] * buf[5 + tap : 5 + tap + BLOCK, :]
        buf[0:8, :] = buf[BLOCK : BLOCK + 8, :]
        return total

    x_pre = conv(x_buf, inner_in, x_taps_ref, x_bias_ref)
    x_pre_ref[...] = x_pre.astype(bf16)
    x = (x_pre * jax.nn.sigmoid(x_pre)).astype(bf16)
    x_ref[...] = x
    s_pre = conv(s_buf, state_in, s_taps_ref, s_bias_ref)
    s_pre_ref[...] = s_pre.astype(bf16)
    bc = (s_pre * jax.nn.sigmoid(s_pre)).astype(bf16)
    bc_ref[...] = bc
    b, c = bc[:, :half], bc[:, half:]

    steps = jax.nn.softplus(step_pre)
    lower = lower_mask(BLOCK)
    cum = select_rows(lower.astype(bf16), steps * rate_ref[...])
    cum_ref[...] = cum
    cum_t = cum.T
    spread = spreader(head_share, head_size)
    cum_x = spread_lanes(cum, spread, 3)
    steps_x = spread_lanes(steps, spread, 2)
    last = cum_x[BLOCK - 1 :, :]
    x_f32 = x.astype(f32)
    stepped = x_f32 * steps_x
    stepped_low = stepped.astype(bf16)

    old = state[...]
    old_low = old.astype(bf16)
    start_ref[0] = old_low
    base = dot(c, old_low) * jnp.exp(cum_x) + skip_ref[...] * x_f32
    weighted = (stepped * jnp.exp(last - cum_x)).astype(bf16)
    state[...] = old * jnp.exp(last) + dot(b, weighted, 0, 0)

    scores = jnp.where(lower, dot(c, b, 1, 1), 0.0)
    mid = BLOCK // 2
    top_scores, low_scores = scores[:mid, :mid], scores[mid:, :]
    pair = LANES // head_size
    lane_head = lax.broadcasted_iota(jnp.int32, (mid, LANES), 1) // head_size
    for first in range(0, head_share, pair):
        at = first * head_size
        values = stepped_low[:, at : at + LANES]
        for k in range(pair):
            top, low = decay_strips(cum, cum_t, first + k)
            top_term = dot((top * top_scores).astype(bf16), values[:mid])
            low_term = dot((low * low_scores).astype(bf16), values)
            if k == 0:
                top_total, low_total = top_term, low_term
            else:
                top_total = jnp.where(lane_head == k, top_term, top_total)
                low_total = jnp.where(lane_head == k, low_term, low_total)
        scanned_ref[:mid, at : at + LANES] = base[:mid, at : at + LANES] + top_total
        scanned_ref[mid:, at : at + LANES] = base[mid:, at : at + LANES] + low_total


def forward_scan(me, pieces, weights, consts, head_share, head_size, rels):
    count, share = pieces[0].shape
    groups = len(pieces)
    features = share * groups
    inner = head_share * head_size
    state2 = consts[3].shape[1]
    blocks = count // BLOCK
    per = lambda width: pl.BlockSpec((BLOCK, width), lambda i: (i, 0))
    outs = [
        (features, bf16),
        (LANES, f32),
        (inner, bf16),
        (inner, bf16),
        (inner, bf16),
        (state2, bf16),
        (state2, bf16),
        (state2, bf16),
        (LANES, f32),
        (LANES, f32),
    ]
    wide = inner + state2 + LANES
    return pl.pallas_call(
        functools.partial(
            forward_kernel, (head_share, head_size, LEN // BLOCK, rels, groups)
        ),
        grid=(blocks,),
        in_specs=[scalar_spec()]
        + [per(share)] * groups
        + [const_spec(a) for a in (*weights, *consts)],
        out_specs=[per(w) for w, _ in outs]
        + [
            pl.BlockSpec((1, state2 // 2, inner), lambda i: (i, 0, 0)),
            per(inner),
            pl.BlockSpec((features, wide), lambda i: (0, 0)),
        ],
        out_shape=[out((count, w), k) for w, k in outs]
        + [
            out((blocks, state2 // 2, inner), bf16),
            out((count, inner), f32),
            out((features, wide), bf16),
        ],
        scratch_shapes=[
            pltpu.VMEM((BLOCK + 8, inner), f32),
            pltpu.VMEM((BLOCK + 8, state2), f32),
            pltpu.VMEM((state2 // 2, inner), f32),
        ],
        compiler_params=params(),
        cost_estimate=cost(16),
    )(me, *pieces, *weights, *consts)


def gate_kernel(sizes, me_ref, *refs):
    z_rels, o_rels, groups = sizes
    cot_refs, refs = refs[:groups], refs[groups:]
    z_first, z_second, o_first, o_second, normed_ref, scanned_ref, gain_ref = refs[:7]
    gate_ref, grad_mid_ref, stats_ref, z_ref, o_ref = refs[7:]
    share = cot_refs[0].shape[1]

    @pl.when(pl.program_id(0) == 0)
    def _():
        held = len(z_rels) // 2
        for i in range(len(z_rels)):
            rows = row_of(me_ref[0] ^ z_rels[i], z_first.shape[1])
            z_ref[rows, :] = z_first[i] if i < held else z_second[i - held]
            rows = row_of(me_ref[0] ^ o_rels[i], z_first.shape[1])
            o_ref[rows, :] = o_first[i] if i < held else o_second[i - held]

    gate_in = dot(normed_ref[...], z_ref[...])
    grad_mid = sum(
        dot(ref[...], o_ref[row_of(me_ref[1] ^ rel, share), :])
        for rel, ref in enumerate(cot_refs)
    )
    gate_ref[...] = gate_in.astype(gate_ref.dtype)
    grad_mid_ref[...] = grad_mid.astype(grad_mid_ref.dtype)
    mixed_in = scanned_ref[...] * (gate_in * jax.nn.sigmoid(gate_in))
    squares = row_sums(mixed_in * mixed_in)
    products = row_sums(grad_mid * gain_ref[...] * mixed_in)
    row = lax.broadcasted_iota(jnp.int32, squares.shape, 0)
    stats_ref[...] = jnp.where(row == 0, squares, products)


def gate(me, cots, weights, normed, scanned, gain, z_rels, o_rels):
    count, share = cots[0].shape
    groups = len(cots)
    features = share * groups
    inner = scanned.shape[1]
    per = lambda width: pl.BlockSpec((BLOCK, width), lambda i: (i, 0))
    whole = pl.BlockSpec((features, inner), lambda i: (0, 0))
    return pl.pallas_call(
        functools.partial(gate_kernel, (z_rels, o_rels, groups)),
        grid=(count // BLOCK,),
        in_specs=[scalar_spec()]
        + [per(share)] * groups
        + [const_spec(a) for a in weights]
        + [per(features), per(inner), const_spec(gain)],
        out_specs=[
            per(inner),
            per(inner),
            pl.BlockSpec((8, BLOCK), lambda i: (0, i)),
            whole,
            whole,
        ],
        out_shape=[
            out((count, inner), f32),
            out((count, inner), bf16),
            out((8, count), f32),
            out((features, inner), bf16),
            out((features, inner), bf16),
        ],
        compiler_params=params(),
        cost_estimate=cost(8),
    )(me, *cots, *weights, normed, scanned, gain)


def mix_kernel(sizes, me_ref, *refs):
    z_rels, o_rels, groups = sizes
    cot_refs, refs = refs[:groups], refs[groups:]
    stats_ref, normed_ref, gate_ref, grad_mid_ref, scanned_ref, o_ref, gain_ref = refs[:7]
    (
        grad_scanned_ref,
        grad_gate_ref,
        out_send,
        out_keep,
        z_send,
        z_keep,
        o_send,
        o_keep,
        gain_grad_ref,
        z_sum,
        o_sum,
    ) = refs[7:]
    inner = gain_ref.shape[1]
    share = out_send.shape[2]

    @pl.when(pl.program_id(0) == 0)
    def _():
        z_sum[...] = jnp.zeros(z_sum.shape, f32)
        o_sum[...] = jnp.zeros(o_sum.shape, f32)
        gain_grad_ref[...] = jnp.zeros(gain_grad_ref.shape, f32)

    stats = stats_ref[...].T
    total = inner * groups
    scale = lax.rsqrt(stats[:, 0:1] / total + epsilon)
    mean = scale * stats[:, 1:2] / total
    gate_in = gate_ref[...]
    sig = jax.nn.sigmoid(gate_in)
    act = gate_in * sig
    scanned = scanned_ref[...]
    mid_hat = scanned * act * scale
    grad_mid = grad_mid_ref[...].astype(f32)
    normed_mid = (mid_hat * gain_ref[...]).astype(bf16)
    gain_grad_ref[0:1, :] += jnp.sum(mid_hat * grad_mid, axis=0, keepdims=True)
    grad_mixed = scale * (grad_mid * gain_ref[...] - mid_hat * mean)
    grad_scanned_ref[...] = (grad_mixed * act).astype(bf16)
    grad_gate = (grad_mixed * scanned * sig * (1.0 + gate_in * (1.0 - sig))).astype(bf16)
    grad_gate_ref[...] = grad_gate
    z_sum[...] += dot(normed_ref[...], grad_gate, 0, 0)
    for rel in range(groups):
        rows = row_of(me_ref[1] ^ rel, share)
        o_sum[rows, :] += dot(cot_refs[rel][...], normed_mid, 0, 0)
        part = dot(normed_mid, o_ref[rows, :], 1, 1).astype(bf16)
        if rel % 2:
            out_send[rel // 2] = part
        else:
            out_keep[rel // 2] = part

    @pl.when(pl.program_id(0) == pl.num_programs(0) - 1)
    def _():
        size = z_send.shape[1]
        for refs_of, total, rels in ((z_send, z_sum, z_rels[0]), (z_keep, z_sum, z_rels[1]), (o_send, o_sum, o_rels[0]), (o_keep, o_sum, o_rels[1])):
            for i, rel in enumerate(rels):
                refs_of[i] = total[row_of(me_ref[0] ^ rel, size), :].astype(bf16)


def mix(me, cots, stats, normed, gate_in, grad_mid, scanned, o_weight, gain, shards, z_rels, o_rels):
    groups = len(cots)
    count, inner = scanned.shape
    features = normed.shape[1]
    share = features // groups
    size = features // shards
    per = lambda width: pl.BlockSpec((BLOCK, width), lambda i: (i, 0))
    parts = pl.BlockSpec((groups // 2, BLOCK, share), lambda i: (0, i, 0))
    early = (shards // 2, size, inner)
    fixed = pl.BlockSpec(early, lambda i: (0, 0, 0))
    return pl.pallas_call(
        functools.partial(mix_kernel, (z_rels, o_rels, groups)),
        grid=(count // BLOCK,),
        in_specs=[scalar_spec()]
        + [per(share)] * groups
        + [
            pl.BlockSpec((8, BLOCK), lambda i: (0, i)),
            per(features),
            per(inner),
            per(inner),
            per(inner),
            const_spec(o_weight),
            const_spec(gain),
        ],
        out_specs=[
            per(inner),
            per(inner),
            parts,
            parts,
            fixed,
            fixed,
            fixed,
            fixed,
            pl.BlockSpec((8, inner), lambda i: (0, 0)),
        ],
        out_shape=[
            out((count, inner), bf16),
            out((count, inner), bf16),
            out((groups // 2, count, share), bf16),
            out((groups // 2, count, share), bf16),
            out(early, bf16),
            out(early, bf16),
            out(early, bf16),
            out(early, bf16),
            out((8, inner), f32),
        ],
        scratch_shapes=[pltpu.VMEM((features, inner), f32)] * 2,
        compiler_params=params(),
        cost_estimate=cost(10),
    )(me, *cots, stats, normed, gate_in, grad_mid, scanned, o_weight, gain)


def backward_kernel(sizes, *refs):
    me_ref = refs[0]
    head_share, head_size, blocks_per_seq, top_block, joined = sizes
    inputs, upper_parts, refs = refs[1:21], refs[21] if joined else None, refs[21 + joined :]
    (
        grad_ref,
        inner_ref,
        x_pre_ref,
        x_ref,
        state_in_ref,
        s_pre_ref,
        bc_ref,
        step_ref,
        cum_ref,
        start_ref,
        x_taps_ref,
        s_taps_ref,
        rate_ref,
        skip_ref,
    ) = inputs[:14]
    given = inputs[14:]
    late_ref, s_parts, *carried_refs = refs
    x_sums, s_sums, small_ref, x_tail, s_tail, state, x_buf, s_buf = carried_refs
    inner = head_share * head_size
    half = bc_ref.shape[1] // 2
    at_block = top_block - pl.program_id(0)

    @pl.when(pl.program_id(0) == 0)
    def _():
        for ref, value in zip((x_sums, s_sums, small_ref, x_tail, s_tail, state), given):
            ref[...] = value[...]

    @pl.when(at_block % blocks_per_seq == blocks_per_seq - 1)
    def _():
        x_tail[...] = jnp.zeros(x_tail.shape, f32)
        s_tail[...] = jnp.zeros(s_tail.shape, f32)
        state[...] = jnp.zeros(state.shape, f32)

    grad_low = grad_ref[...]
    grad = grad_low.astype(f32)
    x = x_ref[...].astype(f32)
    bc = bc_ref[...]
    b, c = bc[:, :half], bc[:, half:]
    step_pre = step_ref[...]
    steps = jax.nn.softplus(step_pre)
    cum = cum_ref[...]
    cum_t = cum.T
    lower = lower_mask(BLOCK)
    row = lax.broadcasted_iota(jnp.int32, (BLOCK, BLOCK), 0)
    col = lax.broadcasted_iota(jnp.int32, (BLOCK, BLOCK), 1)
    spread = spreader(head_share, head_size)
    cum_x = spread_lanes(cum, spread, 3)
    steps_x = spread_lanes(steps, spread, 2)
    last = cum_x[BLOCK - 1 :, :]
    decay_in = jnp.exp(cum_x)
    decay_out = jnp.exp(last - cum_x)
    stepped = x * steps_x
    stepped_low = stepped.astype(bf16)

    old_low = start_ref[0]
    old = old_low.astype(f32)
    later = state[...]
    later_low = later.astype(bf16)
    grad_decayed = grad * decay_in
    grad_decayed_low = grad_decayed.astype(bf16)
    from_later = dot(b, later_low) * decay_out
    carried = dot(c, old_low)
    grad_c = dot(grad_decayed_low, old_low, 1, 1)
    grad_b = dot((stepped * decay_out).astype(bf16), later_low, 1, 1)
    state[...] = later * jnp.exp(last) + dot(c, grad_decayed_low, 0, 0)

    scores = jnp.where(lower, dot(c, b, 1, 1), 0.0)
    mid = BLOCK // 2
    top_scores, low_scores = scores[:mid, :mid], scores[mid:, :]
    pair = LANES // head_size
    lane_head = lax.broadcasted_iota(jnp.int32, (BLOCK, LANES), 1) // head_size
    pick_lane = lax.broadcasted_iota(jnp.int32, (BLOCK, LANES), 1)
    top_sum = jnp.zeros((mid, mid), f32)
    low_sum = jnp.zeros((mid, BLOCK), f32)
    top_cross = jnp.zeros((mid, LANES), f32)
    low_cross = jnp.zeros((mid, LANES), f32)
    all_cross = jnp.zeros((BLOCK, LANES), f32)
    within = []
    for first in range(0, head_share, pair):
        at = first * head_size
        grads = grad_low[:, at : at + LANES]
        values = stepped_low[:, at : at + LANES]
        total = None
        for k in range(pair):
            top, low = decay_strips(cum, cum_t, first + k)
            own = jnp.where(lane_head == k, grads, jnp.zeros_like(grads))
            pick = (pick_lane == first + k).astype(bf16)
            top_products = dot(own[:mid], values[:mid], 1, 1) * top
            low_products = dot(own[mid:], values, 1, 1) * low
            top_sum = top_sum + top_products
            low_sum = low_sum + low_products
            low_term = dot((low * low_scores).astype(bf16), grads[mid:], 0, 0)
            top_term = dot((top * top_scores).astype(bf16), grads[:mid], 0, 0)
            term = low_term + jnp.concatenate([top_term, jnp.zeros_like(top_term)], axis=0)
            total = term if k == 0 else jnp.where(lane_head == k, term, total)
            top_pairs = (top_products * top_scores).astype(bf16)
            low_pairs = (low_products * low_scores).astype(bf16)
            top_cross = top_cross + dot(top_pairs, pick[:mid]) - dot(top_pairs, pick[:mid], 0, 0)
            low_cross = low_cross + dot(low_pairs, pick)
            all_cross = all_cross + dot(low_pairs, pick[mid:], 0, 0)
        within.append(total)
    zeros = jnp.zeros((mid, mid), f32)
    gathered = jnp.concatenate([jnp.concatenate([top_sum, zeros], axis=1), low_sum], axis=0)
    gathered_low = jnp.where(lower, gathered, 0.0).astype(bf16)
    grad_b = grad_b + dot(gathered_low, c, 0, 0)
    grad_c = grad_c + dot(gathered_low, b)
    crossing = jnp.concatenate([top_cross, low_cross], axis=0) - all_cross

    by_x = jnp.concatenate(within, axis=1) + from_later
    fold = lambda values: dot(values.astype(bf16), spread, 1, 1)
    direct = fold(by_x * x)
    into = fold(grad_decayed * carried)
    onward = steps * fold(from_later * x)
    tops = jnp.sum(later * old, axis=0, keepdims=True) * jnp.exp(last)
    spanning = fold(jnp.broadcast_to(tops, (8, inner)))[0:1, :]
    upper = (row <= col).astype(bf16)
    strict = (row > col).astype(bf16)
    by_decay = select_rows(upper, into + crossing, 3) + select_rows(strict, onward, 2) + spanning
    by_step = direct + rate_ref[...] * by_decay
    grad_step = by_step * jax.nn.sigmoid(step_pre)
    small_ref[0:1, :] += jnp.sum(grad_step, axis=0, keepdims=True)
    small_ref[1:2, :] += jnp.sum(steps * by_decay, axis=0, keepdims=True)
    skips = jnp.sum(grad * x, axis=0, keepdims=True)
    small_ref[2:3, :] += sum(
        dot(term, spread, 1, 1) for term in split(jnp.broadcast_to(skips, (8, inner)), 2)
    )[0:1, :]

    def conv_back(buf, tail, by_pre, values, taps_ref, sums):
        buf[0:BLOCK, :] = by_pre
        buf[BLOCK:, :] = tail[...]
        tail[...] = by_pre[0:8, :]
        total = taps_ref[3:4, :] * by_pre
        sums[3:4, :] += jnp.sum(by_pre * values, axis=0, keepdims=True)
        sums[4:5, :] += jnp.sum(by_pre, axis=0, keepdims=True)
        for tap in range(CONV_WIDTH - 1):
            ahead = CONV_WIDTH - 1 - tap
            moved = buf[ahead : ahead + BLOCK, :]
            total = total + taps_ref[tap : tap + 1, :] * moved
            sums[tap : tap + 1, :] += jnp.sum(moved * values, axis=0, keepdims=True)
        return total.astype(bf16)

    by_conv = steps_x * by_x + skip_ref[...] * grad
    by_pre = by_conv * silu_slope(x_pre_ref[...].astype(f32))
    late_ref[:, :inner] = conv_back(
        x_buf, x_tail, by_pre, inner_ref[...].astype(f32), x_taps_ref, x_sums
    )
    by_state = jnp.concatenate([grad_b, grad_c], axis=1) * silu_slope(s_pre_ref[...].astype(f32))
    grad_state = conv_back(
        s_buf, s_tail, by_state, state_in_ref[...].astype(f32), s_taps_ref, s_sums
    )
    late_ref[:, inner : inner + 2 * half] = grad_state
    width = half // 2
    first = lax.broadcasted_iota(jnp.int32, (BLOCK, half), 1) < width
    left, right = grad_state[:, :half], grad_state[:, half:]
    turn = lambda v: jnp.concatenate([v[:, width:], v[:, :width]], axis=1)
    even, odd = jnp.where(first, left, turn(right)), jnp.where(first, turn(left), right)
    own_first, low_side = me_ref[2] == 0, me_ref[1] < 2
    for core, (one, other) in enumerate(((even, odd), (odd, even))):
        half_of = jnp.where(own_first, one, other)
        turned = turn(half_of)
        for side, part in enumerate((jnp.where(low_side, half_of, turned), jnp.where(low_side, turned, half_of))):
            if joined:
                part = jnp.where(first, part, turn(upper_parts[core + 2 * side]))
            s_parts[core + 2 * side] = part
    late_ref[:, inner + 2 * half :] = grad_step.astype(bf16)


def backward_scan(me, part, rows, starts, consts, carry, upper, head_share, head_size):
    first, stop = part
    count, inner = rows[0].shape
    state2 = rows[6].shape[1]
    wide = inner + state2 + LANES
    per = lambda width: pl.BlockSpec((BLOCK, width), lambda i: (stop - 1 - i, 0))
    joined = [] if upper is None else list(upper)[::-1]
    sizes = (head_share, head_size, LEN // BLOCK, stop - 1, len(joined))
    state_parts = pl.BlockSpec((4, BLOCK, state2 // 2), lambda i: (0, stop - first - 1 - i, 0))
    results = pl.pallas_call(
        functools.partial(backward_kernel, sizes),
        grid=(stop - first,),
        in_specs=[scalar_spec()]
        + [per(a.shape[1]) for a in rows]
        + [pl.BlockSpec((1, state2 // 2, inner), lambda i: (stop - 1 - i, 0, 0))]
        + [const_spec(a) for a in (*consts, *carry)]
        + ([state_parts, pl.BlockSpec(memory_space=pl.ANY)] if joined else []),
        out_specs=[per(wide)]
        + [state_parts]
        + [const_spec(a) for a in carry],
        out_shape=[out((count, wide), bf16)]
        + [out((4, (stop - first) * BLOCK, state2 // 2), bf16)]
        + [out(a.shape, f32) for a in carry],
        input_output_aliases={len(rows) + 3 + len(consts) + len(carry): 0} if joined else {},
        scratch_shapes=[
            pltpu.VMEM((BLOCK + 8, inner), f32),
            pltpu.VMEM((BLOCK + 8, state2), f32),
        ],
        compiler_params=params(),
        cost_estimate=cost(12),
    )(me, *rows, starts, *consts, *carry, *joined)
    return results[0], results[1], tuple(results[2:])


def late_kernel(sizes, me_ref, *refs):
    a_rels, b_rels, inner, half = sizes
    late_ref, *state_refs, normed_ref, a_send, a_keep, b_send, b_keep, total = refs

    @pl.when(pl.program_id(0) == 0)
    def _():
        total[...] = jnp.zeros(total.shape, f32)

    rest = inner + 2 * half
    width = LANES // 2
    turn = lambda v: jnp.concatenate([v[:, width:], v[:, :width]], axis=1)
    steps = turn(late_ref[:, rest:])
    state = sum(ref[...].astype(f32) for ref in state_refs).astype(bf16)
    state = jnp.where(pl.program_id(0) < pl.num_programs(0) // 2, state, turn(state))
    first = lax.broadcasted_iota(jnp.int32, (BLOCK, LANES), 1) < width
    both = jnp.concatenate([late_ref[:, :inner], jnp.where(first, state, steps)], axis=1)
    total[...] += dot(normed_ref[...], both, 0, 0)

    @pl.when(pl.program_id(0) == pl.num_programs(0) - 1)
    def _():
        size, cut = a_send.shape[1:]
        for rels, send, keep, columns in (
            (a_rels, a_send, a_keep, slice(0, cut)),
            (b_rels, b_send, b_keep, slice(cut, None)),
        ):
            for to, found in zip((send, keep), rels):
                for i, rel in enumerate(found):
                    to[i] = total[row_of(me_ref[0] ^ rel, size), columns].astype(bf16)


def late_grads(me, late, states, normed, inner, half, shards, a_rels, b_rels):
    count, wide = late.shape
    features = normed.shape[1]
    size = features // shards
    cut = inner // 2
    per = lambda width: pl.BlockSpec((BLOCK, width), lambda i: (i, 0))
    packed = pl.BlockSpec((BLOCK, LANES), lambda i: (i % (count // BLOCK // 2), 0))
    a_part, b_part = (shards // 2, size, cut), (shards // 2, size, inner + LANES - cut)
    outs = [a_part, a_part, b_part, b_part]
    return pl.pallas_call(
        functools.partial(late_kernel, (a_rels, b_rels, inner, half)),
        grid=(count // BLOCK,),
        in_specs=[scalar_spec(), per(wide)] + [packed] * len(states) + [per(features)],
        out_specs=[pl.BlockSpec(dims, lambda i: (0, 0, 0)) for dims in outs],
        out_shape=[out(dims, bf16) for dims in outs],
        scratch_shapes=[pltpu.VMEM((features, inner + LANES), f32)],
        compiler_params=params(),
        cost_estimate=cost(5),
    )(me, late, *states, normed)


def rows_kernel(groups, me_ref, *refs):
    piece_refs, refs = refs[:groups], refs[groups:]
    late_ref, gate_grad_ref, scale_ref, z_ref, weight_ref, gain_ref = refs[:6]
    rows_send, rows_keep, gain_grad_ref, stat_ref = refs[6:]
    share = piece_refs[0].shape[1]

    @pl.when(pl.program_id(0) == 0)
    def _():
        gain_grad_ref[...] = jnp.zeros(gain_grad_ref.shape, f32)

    grad_gate = gate_grad_ref[...]
    late = late_ref[...]
    scale = scale_ref[:, 0:1]
    stat = jnp.zeros((BLOCK, share), f32)
    for rel in range(groups):
        rows = row_of(me_ref[0 + 1] ^ rel, share)
        part = dot(grad_gate, z_ref[rows, :], 1, 1) + dot(late, weight_ref[rows, :], 1, 1)
        to = rows_send if rel % 2 else rows_keep
        to[rel // 2] = part.astype(bf16)
        product = piece_refs[rel][...].astype(f32) * scale * part
        gain_grad_ref[0:1, rows] += jnp.sum(product, axis=0, keepdims=True)
        stat = stat + product * gain_ref[:, rows]
    stat_ref[...] = row_sums(stat)


def row_grads(me, pieces, late, grad_gate, scale, z_all, weight, gain):
    count, share = pieces[0].shape
    groups = len(pieces)
    features = share * groups
    per = lambda width: pl.BlockSpec((BLOCK, width), lambda i: (i, 0))
    parts = pl.BlockSpec((groups // 2, BLOCK, share), lambda i: (0, i, 0))
    return pl.pallas_call(
        functools.partial(rows_kernel, groups),
        grid=(count // BLOCK,),
        in_specs=[scalar_spec()]
        + [per(a.shape[1]) for a in (*pieces, late, grad_gate, scale)]
        + [const_spec(a) for a in (z_all, weight, gain)],
        out_specs=[
            parts,
            parts,
            pl.BlockSpec((8, features), lambda i: (0, 0)),
            pl.BlockSpec((8, BLOCK), lambda i: (0, i)),
        ],
        out_shape=[
            out((groups // 2, count, share), bf16),
            out((groups // 2, count, share), bf16),
            out((8, features), f32),
            out((8, count), f32),
        ],
        compiler_params=params(),
        cost_estimate=cost(6),
    )(me, *pieces, late, grad_gate, scale, z_all, weight, gain)


def swap(value, axis, step):
    count = lax.axis_size(axis)
    return lax.ppermute(value, axis, [(i, i ^ step) for i in range(count)])


def steps_of(axis):
    found = []
    while 2 ** len(found) < lax.axis_size(axis):
        found.append(2 ** len(found))
    return found


def rels_of(order):
    rels = [0]
    for step in order:
        rels = rels + [rel ^ step for rel in rels]
    return rels


def halves_of(order):
    rels = rels_of(order[:0:-1])
    return [rel ^ order[0] for rel in rels], rels


def gather_steps(value, axis, order):
    held = value[None]
    for i, step in enumerate(order):
        held, got = yield held, swap(held, axis, step)
        if i < len(order) - 1:
            held = jnp.concatenate([held, got], axis=0)


def reduce_steps(send, keep, axis, order):
    for i, step in enumerate(order):
        keep, got = yield keep, swap(send, axis, step)
        if i < len(order) - 1:
            total = keep.astype(f32) + got.astype(f32)
            mid = total.shape[0] // 2
            keep, send = total[:mid], total[mid:].astype(bf16)


def pair_steps(send, keep, axis, order):
    keep, got = yield keep, swap(send, axis, order[0])
    send = (keep[1:].astype(f32) + got[1:].astype(f32)).astype(bf16)
    yield (keep, got), swap(send, axis, order[1])


def sum_steps(value, axis, order):
    for step in order:
        value, got = yield value, swap(value, axis, step)
        value = value + got


class Exchange:
    def __init__(self, steps, left=0):
        self.steps, self.value, self.ended, self.left = steps, None, False, left

    def advance(self):
        self.left -= 1
        try:
            self.value = self.steps.send(self.value)
        except StopIteration:
            self.ended = True

    def total(self):
        keep, got = self.value
        return keep.astype(f32) + got.astype(f32)


def phase(exchanges, beside=()):
    values, beside = lax.optimization_barrier(([e.value for e in exchanges], beside))
    for exchange, value in zip(exchanges, values):
        exchange.value = value
    return beside


def finish(exchanges, jobs):
    moving, results = exchanges, [None] * len(jobs)
    while moving:
        for exchange in moving:
            exchange.advance()
        moving = [exchange for exchange in moving if not exchange.ended]
        new = [i for i, job in enumerate(jobs) if job[0].ended and results[i] is None]
        made = [jobs[i][1]() for i in new]
        if any(exchange.left > 0 for exchange in moving):
            made = phase(moving, made)
        for i, result in zip(new, made):
            results[i] = result
    return results


def body(
    tokens,
    z_weight,
    x_weight,
    bc_weight,
    dt_weight,
    out_weight,
    norm_gain,
    gate_gain,
    x_conv_weight,
    x_conv_bias,
    bc_conv_weight,
    bc_conv_bias,
    step_bias,
    decay_log,
    skip_gain,
    cotangent,
):
    head_index = lax.axis_index("heads")
    shard_index = lax.axis_index("shard")
    groups = lax.axis_size("heads")
    shards = lax.axis_size("shard")
    row_count, feature_share = tokens.shape
    feature_total = feature_share * groups
    size, inner_share = z_weight.shape
    head_share = dt_weight.shape[1]
    head_size = inner_share // head_share
    state_width = bc_weight.shape[1]
    half = state_width // 2
    near = steps_of("shard")
    far = near[::-1]
    rels = rels_of(far)
    core = head_index % 2
    me = jnp.stack([shard_index, head_index, core]).astype(jnp.int32)
    step_pad = LANES - head_share

    own_half = lax.dynamic_slice_in_dim(bc_weight, core * half, half, 1)
    scan_weight = jnp.concatenate(
        [x_weight, own_half, jnp.pad(dt_weight, ((0, 0), (0, step_pad)))], axis=1
    )
    o_order = near[:1] + far[:-1]
    scan_x = Exchange(gather_steps(scan_weight, "shard", far))
    z_x = Exchange(gather_steps(z_weight, "shard", far))
    o_x = Exchange(gather_steps(out_weight.T, "shard", o_order), len(far))
    last = len(far) - 1
    cut = lambda v: v[:, :, inner_share : inner_share + half]
    for i in range(len(far)):
        scan_x.advance()
        moving = [scan_x]
        if i > 0:
            z_x.advance()
            moving.append(z_x)
        if i != 1:
            o_x.advance()
            moving.append(o_x)
        if i == 0:
            beside = (swap(tokens, "heads", 2), swap(tokens, "heads", 1))
            tokens_across, tokens_near, z_from, cot_from = phase(
                moving, (*beside, z_weight, cotangent)
            )
            z_x = Exchange(gather_steps(z_from, "shard", far), len(far))
        elif i == last:
            beside = (
                swap(tokens_across, "heads", 1),
                swap(cot_from, "heads", 2),
                swap(cut(scan_x.value[0]), "heads", 1),
            )
            tokens_last, cot_across, other_held = phase(moving, beside)
        else:
            (cot_from,) = phase(moving, (cot_from,))
    scan_held, scan_got = scan_x.value
    token_parts = [tokens, tokens_near, tokens_across, tokens_last]
    other_got = swap(cut(scan_got), "heads", 1)

    pad_lanes = lambda v: jnp.pad(v, (0, step_pad))[None]
    rate = pad_lanes(-jnp.exp(decay_log))
    skip_x = jnp.repeat(skip_gain, head_size)[None]
    z_x.advance()
    o_x.advance()
    cot_near, cot_last = swap(cot_from, "heads", 1), swap(cot_across, "heads", 1)
    scan = forward_scan(
        me,
        token_parts,
        (scan_held, scan_got, other_held, other_got),
        (
            norm_gain[None],
            x_conv_weight,
            x_conv_bias[None],
            bc_conv_weight,
            bc_conv_bias[None],
            pad_lanes(step_bias),
            rate,
            skip_x,
        ),
        head_share,
        head_size,
        rels,
    )

    (
        normed,
        scale_in,
        inner_in,
        x_pre,
        x,
        state_in,
        s_pre,
        bc,
        step_pre,
        cum,
        starts,
        scanned,
        scan_weight_all,
    ), (cot_near, cot_last) = phase([z_x, o_x], (scan, (cot_near, cot_last)))
    finish([z_x, o_x], [])
    cot_parts = [cotangent, cot_near, cot_across, cot_last]

    gain_row = gate_gain[None]
    gate_in, grad_mid, stats, z_all, o_all = gate(
        me, cot_parts, (*z_x.value, *o_x.value), normed, scanned, gain_row, rels, rels_of(o_order)
    )
    for step in (1, 2):
        stats = stats + swap(stats, "heads", step)

    send_rels, keep_rels = halves_of(near)
    o_sums = near[1:] + near[:1]
    (
        grad_scanned,
        grad_gate,
        out_send,
        out_keep,
        z_send,
        z_keep,
        o_send,
        o_keep,
        gate_gain_grad,
    ) = mix(
        me, cot_parts, stats, normed, gate_in, grad_mid, scanned, o_all, gain_row,
        shards, (send_rels, keep_rels), halves_of(o_sums),
    )
    z_x = Exchange(reduce_steps(z_send, z_keep, "shard", near), len(near))
    o_x = Exchange(reduce_steps(o_send, o_keep, "shard", o_sums), len(near))
    out_x = Exchange(reduce_steps(out_send, out_keep, "heads", [1, 2]))

    blocks = row_count // BLOCK
    carry = tuple(
        jnp.zeros(dims, f32)
        for dims in (
            (8, inner_share),
            (8, state_width),
            (8, LANES),
            (8, inner_share),
            (8, state_width),
            (half, inner_share),
        )
    )
    scan_rows = (grad_scanned, inner_in, x_pre, x, state_in, s_pre, bc, step_pre, cum)
    scan_consts = (x_conv_weight, bc_conv_weight, rate, skip_x)
    sizes = (head_share, head_size)
    quarter = half // 2
    for exchange in (z_x, o_x, out_x):
        exchange.advance()
    late, s_upper, carry = phase(
        [z_x, o_x, out_x],
        backward_scan(me, (blocks // 2, blocks), scan_rows, starts, scan_consts, carry, None, *sizes),
    )
    for exchange in (z_x, o_x, out_x):
        exchange.advance()
    late, state_parts, carry = phase(
        [z_x, o_x, out_x],
        backward_scan(
            me, (0, blocks // 2), scan_rows, starts, scan_consts, carry, (late, s_upper), *sizes
        ),
    )
    x_sums, s_sums, small = carry[:3]
    (rows_send, rows_keep, gain_grad, stat), state_got = phase(
        [],
        (
            row_grads(
                me, token_parts, late, grad_gate, scale_in, z_all, scan_weight_all, norm_gain[None]
            ),
            [swap(state_parts[step], "heads", step) for step in (1, 2, 3)],
        ),
    )

    b_sums = near[1:] + near[:1]
    rows_x = Exchange(pair_steps(rows_send, rows_keep, "heads", [1, 2]))
    by_heads = jnp.concatenate([gain_grad[0], stat[0], s_sums[: CONV_WIDTH + 1].reshape(-1)])
    rows_x.advance()
    (a_send, a_keep, b_send, b_keep), by_heads, got = phase(
        [rows_x, z_x, o_x],
        (
            late_grads(
                me, late, (state_parts[0], *state_got), normed, inner_share, half, shards, halves_of(near), halves_of(b_sums)
            ),
            by_heads,
            [swap(by_heads, "heads", step) for step in (1, 2, 3)],
        ),
    )
    a_x = Exchange(reduce_steps(a_send, a_keep, "shard", near), len(near))
    b_x = Exchange(reduce_steps(b_send, b_keep, "shard", b_sums), len(near))
    by_heads = (by_heads + got[0]) + (got[1] + got[2])
    local = jnp.concatenate(
        [
            gate_gain_grad[0],
            x_sums[: CONV_WIDTH + 1].reshape(-1),
            small[0, :head_share],
            small[1, :head_share],
            small[2, :head_share],
        ]
    )
    summed = jnp.concatenate(
        [
            lax.dynamic_slice_in_dim(by_heads, head_index * feature_share, feature_share, 0),
            by_heads[feature_total + row_count :],
            local,
        ]
    )
    small_x = Exchange(sum_steps(summed, "shard", near), len(near))
    for exchange in (a_x, b_x, rows_x, small_x, z_x):
        exchange.advance()
    mixed = (tokens.astype(f32) + out_x.total()[0]).astype(bf16)
    norm_stat = by_heads[feature_total : feature_total + row_count]
    mixed, norm_stat = phase([a_x, b_x, rows_x, small_x, z_x], (mixed, norm_stat))
    scale = scale_in[:, :1]
    gain_share = lax.dynamic_slice_in_dim(norm_gain, head_index * feature_share, feature_share, 0)

    def token_grads():
        tokens_hat = tokens.astype(f32) * scale
        (first, second), third = rows_x.value
        total = first[0].astype(f32) + second[0].astype(f32) + third[0].astype(f32)
        scaled = total * gain_share - tokens_hat * (norm_stat / feature_total)[:, None]
        return (cotangent.astype(f32) + scale * scaled).astype(bf16)

    tokens_grad, z_sum, o_sum, a_sum, b_sum, summed = finish(
        [o_x, a_x, b_x, rows_x, small_x, z_x],
        [
            (rows_x, token_grads),
            (z_x, lambda: z_x.total()[0]),
            (o_x, lambda: o_x.total()[0].T),
            (a_x, lambda: a_x.total()[0]),
            (b_x, lambda: b_x.total()[0]),
            (small_x, small_x.total),
        ],
    )
    steps_at = inner_share - a_sum.shape[1]

    cuts, at = [], 0
    taps = CONV_WIDTH + 1
    for count in (feature_share, taps * state_width, inner_share, taps * inner_share) + (head_share,) * 3:
        cuts.append(summed[at : at + count])
        at += count
    bc_taps = cuts[1].reshape(taps, state_width)
    x_taps = cuts[3].reshape(taps, inner_share)
    return (
        mixed,
        tokens_grad,
        z_sum,
        jnp.concatenate([a_sum, b_sum[:, :steps_at]], axis=1),
        b_sum[:, steps_at : steps_at + quarter],
        b_sum[:, steps_at + LANES // 2 : steps_at + LANES // 2 + head_share],
        o_sum,
        cuts[0],
        cuts[2],
        x_taps[:CONV_WIDTH],
        x_taps[CONV_WIDTH],
        bc_taps[:CONV_WIDTH],
        bc_taps[CONV_WIDTH],
        cuts[4],
        cuts[5] * rate[0, :head_share],
        cuts[6],
    )


def solution(mesh):
    placed = (
        P("shard", "heads"),
        P("shard", "heads"),
        P("shard", "heads"),
        P("shard", None),
        P("shard", "heads"),
        P("heads", "shard"),
        P(),
        P("heads"),
        P(None, "heads"),
        P("heads"),
        P(),
        P(),
        P("heads"),
        P("heads"),
        P("heads"),
        P("shard", "heads"),
    )
    return jax.shard_map(
        body,
        mesh=mesh,
        in_specs=placed,
        out_specs=(
            P("shard", "heads"),
            P("shard", "heads"),
            P("shard", "heads"),
            P("shard", "heads"),
            P("shard", "heads"),
            P("shard", "heads"),
            P("heads", "shard"),
            P("heads"),
            P("heads"),
            P(None, "heads"),
            P("heads"),
            P(),
            P(),
            P("heads"),
            P("heads"),
            P("heads"),
        ),
        check_vma=False,
    )
```

```python
import functools

import jax
import jax.numpy as jnp
from jax import lax
from jax.experimental import pallas as pl
from jax.experimental.pallas import tpu as pltpu
from jax.sharding import PartitionSpec as P

CONV_WIDTH = 4
LEN = 1024
BLOCK = 256
ROWS = 512
LANES = 128

epsilon = 1e-05
highest = lax.Precision.HIGHEST
f32 = jnp.float32
bf16 = jnp.bfloat16
VMEM_LIMIT = 53 * 1024 * 1024


def dot(left, right, left_dim=1, right_dim=0, precision=None):
    return lax.dot_general(
        left,
        right,
        (((left_dim,), (right_dim,)), ((), ())),
        precision=precision,
        preferred_element_type=f32,
    )


def spreader(head_share, head_size):
    row = lax.broadcasted_iota(jnp.int32, (LANES, head_share * head_size), 0)
    head = lax.broadcasted_iota(jnp.int32, (LANES, head_share * head_size), 1) // head_size
    return (row == head).astype(bf16)


def lower_mask(size):
    row = lax.broadcasted_iota(jnp.int32, (size, size), 0)
    col = lax.broadcasted_iota(jnp.int32, (size, size), 1)
    return row >= col


def const_spec(array):
    return pl.BlockSpec(array.shape, lambda i: (0,) * array.ndim)


def scalar_spec():
    return pl.BlockSpec(memory_space=pltpu.SMEM)


def cost(micros):
    return pl.CostEstimate(flops=int(micros * 1e9), bytes_accessed=0, transcendentals=0)


def params():
    return pltpu.CompilerParams(vmem_limit_bytes=VMEM_LIMIT)


def out(shape, kind):
    return jax.ShapeDtypeStruct(shape, kind)


def row_of(index, size):
    return pl.ds(pl.multiple_of(index * size, size), size)


def silu_slope(values):
    sig = jax.nn.sigmoid(values)
    return sig * (1.0 + values * (1.0 - sig))


def row_sums(values):
    return dot(jnp.ones((8, values.shape[1]), bf16), values.astype(bf16), 1, 1)


def split(values, count):
    terms = []
    for _ in range(count):
        terms.append(values.astype(bf16))
        values = values - terms[-1].astype(f32)
    return terms


def select_rows(ones, values, count=3):
    return sum(dot(ones, term) for term in split(values, count))


def spread_lanes(values, spread, count):
    return sum(dot(term, spread) for term in split(values, count))


def decay_strips(cum, cum_t, head):
    mid = BLOCK // 2
    row = cum_t[head : head + 1, :]
    top = jnp.exp(jnp.minimum(cum[:mid, head : head + 1] - row[:, :mid], 0.0))
    low = jnp.exp(jnp.minimum(cum[mid:, head : head + 1] - row, 0.0))
    return top, low


def forward_kernel(
    sizes,
    me_ref,
    *refs,
):
    head_share, head_size, blocks_per_seq, rels, groups = sizes
    piece_refs, refs = refs[:groups], refs[groups:]
    (
        first_ref,
        second_ref,
        other_first,
        other_second,
        gain_ref,
        x_taps_ref,
        x_bias_ref,
        s_taps_ref,
        s_bias_ref,
        step_bias_ref,
        rate_ref,
        skip_ref,
        normed_ref,
        scale_ref,
        inner_ref,
        x_pre_ref,
        x_ref,
        state_in_ref,
        s_pre_ref,
        bc_ref,
        step_ref,
        cum_ref,
        start_ref,
        scanned_ref,
        weight_ref,
        x_buf,
        s_buf,
        state,
    ) = refs
    inner = head_share * head_size
    half = s_bias_ref.shape[1] // 2
    share = piece_refs[0].shape[1]

    @pl.when(pl.program_id(0) == 0)
    def _():
        own_first = me_ref[2] == 0
        for i, rel in enumerate(rels):
            rows = row_of(me_ref[0] ^ rel, first_ref.shape[1])
            held = len(rels) // 2
            part = first_ref[i] if i < held else second_ref[i - held]
            mine = part[:, inner : inner + half]
            others = other_first[i] if i < held else other_second[i - held]
            weight_ref[rows, :inner] = part[:, :inner]
            weight_ref[rows, inner : inner + half] = jnp.where(own_first, mine, others)
            weight_ref[rows, inner + half : inner + 2 * half] = jnp.where(own_first, others, mine)
            weight_ref[rows, inner + 2 * half :] = part[:, inner + half :]

    @pl.when(pl.program_id(0) % blocks_per_seq == 0)
    def _():
        x_buf[0:8, :] = jnp.zeros((8, inner), f32)
        s_buf[0:8, :] = jnp.zeros((8, 2 * half), f32)
        state[...] = jnp.zeros(state.shape, f32)

    pieces = [ref[...].astype(f32) for ref in piece_refs]
    squares = pieces[0] * pieces[0]
    for piece in pieces[1:]:
        squares = squares + piece * piece
    mean = jnp.sum(squares, axis=-1, keepdims=True) / (share * groups)
    scale = lax.rsqrt(mean + epsilon)
    scale_ref[...] = jnp.broadcast_to(scale, scale_ref.shape)
    for rel, piece in enumerate(pieces):
        at = row_of(me_ref[1] ^ rel, share)
        normed_ref[:, at] = (piece * scale * gain_ref[:, at]).astype(bf16)
    projected = dot(normed_ref[...], weight_ref[...])
    inner_in = projected[:, :inner]
    state_in = projected[:, inner : inner + 2 * half]
    step_pre = projected[:, inner + 2 * half :] + step_bias_ref[...]
    inner_ref[...] = inner_in.astype(bf16)
    state_in_ref[...] = state_in.astype(bf16)
    step_ref[...] = step_pre

    def conv(buf, values, taps_ref, bias_ref):
        buf[8 : 8 + BLOCK, :] = values
        total = bias_ref[...] + taps_ref[3:4, :] * values
        for tap in range(CONV_WIDTH - 1):
            total = total + taps_ref[tap : tap + 1, :] * buf[5 + tap : 5 + tap + BLOCK, :]
        buf[0:8, :] = buf[BLOCK : BLOCK + 8, :]
        return total

    x_pre = conv(x_buf, inner_in, x_taps_ref, x_bias_ref)
    x_pre_ref[...] = x_pre.astype(bf16)
    x = (x_pre * jax.nn.sigmoid(x_pre)).astype(bf16)
    x_ref[...] = x
    s_pre = conv(s_buf, state_in, s_taps_ref, s_bias_ref)
    s_pre_ref[...] = s_pre.astype(bf16)
    bc = (s_pre * jax.nn.sigmoid(s_pre)).astype(bf16)
    bc_ref[...] = bc
    b, c = bc[:, :half], bc[:, half:]

    steps = jax.nn.softplus(step_pre)
    lower = lower_mask(BLOCK)
    cum = select_rows(lower.astype(bf16), steps * rate_ref[...])
    cum_ref[...] = cum
    cum_t = cum.T
    spread = spreader(head_share, head_size)
    cum_x = spread_lanes(cum, spread, 3)
    steps_x = spread_lanes(steps, spread, 2)
    last = cum_x[BLOCK - 1 :, :]
    x_f32 = x.astype(f32)
    stepped = x_f32 * steps_x
    stepped_low = stepped.astype(bf16)

    old = state[...]
    old_low = old.astype(bf16)
    start_ref[0] = old_low
    base = dot(c, old_low) * jnp.exp(cum_x) + skip_ref[...] * x_f32
    weighted = (stepped * jnp.exp(last - cum_x)).astype(bf16)
    state[...] = old * jnp.exp(last) + dot(b, weighted, 0, 0)

    scores = jnp.where(lower, dot(c, b, 1, 1), 0.0)
    mid = BLOCK // 2
    top_scores, low_scores = scores[:mid, :mid], scores[mid:, :]
    pair = LANES // head_size
    lane_head = lax.broadcasted_iota(jnp.int32, (mid, LANES), 1) // head_size
    for first in range(0, head_share, pair):
        at = first * head_size
        values = stepped_low[:, at : at + LANES]
        for k in range(pair):
            top, low = decay_strips(cum, cum_t, first + k)
            top_term = dot((top * top_scores).astype(bf16), values[:mid])
            low_term = dot((low * low_scores).astype(bf16), values)
            if k == 0:
                top_total, low_total = top_term, low_term
            else:
                top_total = jnp.where(lane_head == k, top_term, top_total)
                low_total = jnp.where(lane_head == k, low_term, low_total)
        scanned_ref[:mid, at : at + LANES] = base[:mid, at : at + LANES] + top_total
        scanned_ref[mid:, at : at + LANES] = base[mid:, at : at + LANES] + low_total


def forward_scan(me, pieces, weights, consts, head_share, head_size, rels):
    count, share = pieces[0].shape
    groups = len(pieces)
    features = share * groups
    inner = head_share * head_size
    state2 = consts[3].shape[1]
    blocks = count // BLOCK
    per = lambda width: pl.BlockSpec((BLOCK, width), lambda i: (i, 0))
    outs = [
        (features, bf16),
        (LANES, f32),
        (inner, bf16),
        (inner, bf16),
        (inner, bf16),
        (state2, bf16),
        (state2, bf16),
        (state2, bf16),
        (LANES, f32),
        (LANES, f32),
    ]
    wide = inner + state2 + LANES
    return pl.pallas_call(
        functools.partial(
            forward_kernel, (head_share, head_size, LEN // BLOCK, rels, groups)
        ),
        grid=(blocks,),
        in_specs=[scalar_spec()]
        + [per(share)] * groups
        + [const_spec(a) for a in (*weights, *consts)],
        out_specs=[per(w) for w, _ in outs]
        + [
            pl.BlockSpec((1, state2 // 2, inner), lambda i: (i, 0, 0)),
            per(inner),
            pl.BlockSpec((features, wide), lambda i: (0, 0)),
        ],
        out_shape=[out((count, w), k) for w, k in outs]
        + [
            out((blocks, state2 // 2, inner), bf16),
            out((count, inner), f32),
            out((features, wide), bf16),
        ],
        scratch_shapes=[
            pltpu.VMEM((BLOCK + 8, inner), f32),
            pltpu.VMEM((BLOCK + 8, state2), f32),
            pltpu.VMEM((state2 // 2, inner), f32),
        ],
        compiler_params=params(),
        cost_estimate=cost(16),
    )(me, *pieces, *weights, *consts)


def gate_kernel(sizes, me_ref, *refs):
    z_rels, o_rels, groups = sizes
    cot_refs, refs = refs[:groups], refs[groups:]
    z_first, z_second, o_first, o_second, normed_ref, scanned_ref, gain_ref = refs[:7]
    gate_ref, grad_mid_ref, stats_ref, z_ref, o_ref = refs[7:]
    share = cot_refs[0].shape[1]

    @pl.when(pl.program_id(0) == 0)
    def _():
        held = len(z_rels) // 2
        for i in range(len(z_rels)):
            rows = row_of(me_ref[0] ^ z_rels[i], z_first.shape[1])
            z_ref[rows, :] = z_first[i] if i < held else z_second[i - held]
            rows = row_of(me_ref[0] ^ o_rels[i], z_first.shape[1])
            o_ref[rows, :] = o_first[i] if i < held else o_second[i - held]

    gate_in = dot(normed_ref[...], z_ref[...])
    grad_mid = sum(
        dot(ref[...], o_ref[row_of(me_ref[1] ^ rel, share), :])
        for rel, ref in enumerate(cot_refs)
    )
    gate_ref[...] = gate_in.astype(gate_ref.dtype)
    grad_mid_ref[...] = grad_mid.astype(grad_mid_ref.dtype)
    mixed_in = scanned_ref[...] * (gate_in * jax.nn.sigmoid(gate_in))
    squares = row_sums(mixed_in * mixed_in)
    products = row_sums(grad_mid * gain_ref[...] * mixed_in)
    row = lax.broadcasted_iota(jnp.int32, squares.shape, 0)
    stats_ref[...] = jnp.where(row == 0, squares, products)


def gate(me, cots, weights, normed, scanned, gain, z_rels, o_rels):
    count, share = cots[0].shape
    groups = len(cots)
    features = share * groups
    inner = scanned.shape[1]
    per = lambda width: pl.BlockSpec((ROWS, width), lambda i: (i, 0))
    whole = pl.BlockSpec((features, inner), lambda i: (0, 0))
    return pl.pallas_call(
        functools.partial(gate_kernel, (z_rels, o_rels, groups)),
        grid=(count // ROWS,),
        in_specs=[scalar_spec()]
        + [per(share)] * groups
        + [const_spec(a) for a in weights]
        + [per(features), per(inner), const_spec(gain)],
        out_specs=[
            per(inner),
            per(inner),
            pl.BlockSpec((8, ROWS), lambda i: (0, i)),
            whole,
            whole,
        ],
        out_shape=[
            out((count, inner), f32),
            out((count, inner), bf16),
            out((8, count), f32),
            out((features, inner), bf16),
            out((features, inner), bf16),
        ],
        compiler_params=params(),
        cost_estimate=cost(8),
    )(me, *cots, *weights, normed, scanned, gain)


def mix_kernel(sizes, me_ref, *refs):
    z_rels, o_rels, groups = sizes
    cot_refs, refs = refs[:groups], refs[groups:]
    stats_ref, normed_ref, gate_ref, grad_mid_ref, scanned_ref, o_ref, gain_ref = refs[:7]
    (
        grad_scanned_ref,
        grad_gate_ref,
        out_send,
        out_keep,
        z_send,
        z_keep,
        o_send,
        o_keep,
        gain_grad_ref,
        z_sum,
        o_sum,
    ) = refs[7:]
    inner = gain_ref.shape[1]
    share = out_send.shape[2]

    @pl.when(pl.program_id(0) == 0)
    def _():
        z_sum[...] = jnp.zeros(z_sum.shape, f32)
        o_sum[...] = jnp.zeros(o_sum.shape, f32)
        gain_grad_ref[...] = jnp.zeros(gain_grad_ref.shape, f32)

    stats = stats_ref[...].T
    total = inner * groups
    scale = lax.rsqrt(stats[:, 0:1] / total + epsilon)
    mean = scale * stats[:, 1:2] / total
    gate_in = gate_ref[...]
    sig = jax.nn.sigmoid(gate_in)
    act = gate_in * sig
    scanned = scanned_ref[...]
    mid_hat = scanned * act * scale
    grad_mid = grad_mid_ref[...].astype(f32)
    normed_mid = (mid_hat * gain_ref[...]).astype(bf16)
    gain_grad_ref[0:1, :] += jnp.sum(mid_hat * grad_mid, axis=0, keepdims=True)
    grad_mixed = scale * (grad_mid * gain_ref[...] - mid_hat * mean)
    grad_scanned_ref[...] = (grad_mixed * act).astype(bf16)
    grad_gate = (grad_mixed * scanned * sig * (1.0 + gate_in * (1.0 - sig))).astype(bf16)
    grad_gate_ref[...] = grad_gate
    z_sum[...] += dot(normed_ref[...], grad_gate, 0, 0)
    for rel in range(groups):
        rows = row_of(me_ref[1] ^ rel, share)
        o_sum[rows, :] += dot(cot_refs[rel][...], normed_mid, 0, 0)
        part = dot(normed_mid, o_ref[rows, :], 1, 1).astype(bf16)
        if rel % 2:
            out_send[rel // 2] = part
        else:
            out_keep[rel // 2] = part

    @pl.when(pl.program_id(0) == pl.num_programs(0) - 1)
    def _():
        size = z_send.shape[1]
        for refs_of, total, rels in ((z_send, z_sum, z_rels[0]), (z_keep, z_sum, z_rels[1]), (o_send, o_sum, o_rels[0]), (o_keep, o_sum, o_rels[1])):
            for i, rel in enumerate(rels):
                refs_of[i] = total[row_of(me_ref[0] ^ rel, size), :].astype(bf16)


def mix(me, cots, stats, normed, gate_in, grad_mid, scanned, o_weight, gain, shards, z_rels, o_rels):
    groups = len(cots)
    count, inner = scanned.shape
    features = normed.shape[1]
    share = features // groups
    size = features // shards
    per = lambda width: pl.BlockSpec((BLOCK, width), lambda i: (i, 0))
    parts = pl.BlockSpec((groups // 2, BLOCK, share), lambda i: (0, i, 0))
    early = (shards // 2, size, inner)
    fixed = pl.BlockSpec(early, lambda i: (0, 0, 0))
    return pl.pallas_call(
        functools.partial(mix_kernel, (z_rels, o_rels, groups)),
        grid=(count // BLOCK,),
        in_specs=[scalar_spec()]
        + [per(share)] * groups
        + [
            pl.BlockSpec((8, BLOCK), lambda i: (0, i)),
            per(features),
            per(inner),
            per(inner),
            per(inner),
            const_spec(o_weight),
            const_spec(gain),
        ],
        out_specs=[
            per(inner),
            per(inner),
            parts,
            parts,
            fixed,
            fixed,
            fixed,
            fixed,
            pl.BlockSpec((8, inner), lambda i: (0, 0)),
        ],
        out_shape=[
            out((count, inner), bf16),
            out((count, inner), bf16),
            out((groups // 2, count, share), bf16),
            out((groups // 2, count, share), bf16),
            out(early, bf16),
            out(early, bf16),
            out(early, bf16),
            out(early, bf16),
            out((8, inner), f32),
        ],
        scratch_shapes=[pltpu.VMEM((features, inner), f32)] * 2,
        compiler_params=params(),
        cost_estimate=cost(10),
    )(me, *cots, stats, normed, gate_in, grad_mid, scanned, o_weight, gain)


def backward_kernel(sizes, *refs):
    me_ref = refs[0]
    head_share, head_size, blocks_per_seq, top_block, joined = sizes
    inputs, upper_parts, refs = refs[1:21], refs[21] if joined else None, refs[21 + joined :]
    (
        grad_ref,
        inner_ref,
        x_pre_ref,
        x_ref,
        state_in_ref,
        s_pre_ref,
        bc_ref,
        step_ref,
        cum_ref,
        start_ref,
        x_taps_ref,
        s_taps_ref,
        rate_ref,
        skip_ref,
    ) = inputs[:14]
    given = inputs[14:]
    late_ref, s_parts, *carried_refs = refs
    x_sums, s_sums, small_ref, x_tail, s_tail, state, x_buf, s_buf = carried_refs
    inner = head_share * head_size
    half = bc_ref.shape[1] // 2
    at_block = top_block - pl.program_id(0)

    @pl.when(pl.program_id(0) == 0)
    def _():
        for ref, value in zip((x_sums, s_sums, small_ref, x_tail, s_tail, state), given):
            ref[...] = value[...]

    @pl.when(at_block % blocks_per_seq == blocks_per_seq - 1)
    def _():
        x_tail[...] = jnp.zeros(x_tail.shape, f32)
        s_tail[...] = jnp.zeros(s_tail.shape, f32)
        state[...] = jnp.zeros(state.shape, f32)

    grad_low = grad_ref[...]
    grad = grad_low.astype(f32)
    x = x_ref[...].astype(f32)
    bc = bc_ref[...]
    b, c = bc[:, :half], bc[:, half:]
    step_pre = step_ref[...]
    steps = jax.nn.softplus(step_pre)
    cum = cum_ref[...]
    cum_t = cum.T
    lower = lower_mask(BLOCK)
    row = lax.broadcasted_iota(jnp.int32, (BLOCK, BLOCK), 0)
    col = lax.broadcasted_iota(jnp.int32, (BLOCK, BLOCK), 1)
    spread = spreader(head_share, head_size)
    cum_x = spread_lanes(cum, spread, 3)
    steps_x = spread_lanes(steps, spread, 2)
    last = cum_x[BLOCK - 1 :, :]
    decay_in = jnp.exp(cum_x)
    decay_out = jnp.exp(last - cum_x)
    stepped = x * steps_x
    stepped_low = stepped.astype(bf16)

    old_low = start_ref[0]
    old = old_low.astype(f32)
    later = state[...]
    later_low = later.astype(bf16)
    grad_decayed = grad * decay_in
    grad_decayed_low = grad_decayed.astype(bf16)
    from_later = dot(b, later_low) * decay_out
    carried = dot(c, old_low)
    grad_c = dot(grad_decayed_low, old_low, 1, 1)
    grad_b = dot((stepped * decay_out).astype(bf16), later_low, 1, 1)
    state[...] = later * jnp.exp(last) + dot(c, grad_decayed_low, 0, 0)

    scores = jnp.where(lower, dot(c, b, 1, 1), 0.0)
    mid = BLOCK // 2
    top_scores, low_scores = scores[:mid, :mid], scores[mid:, :]
    pair = LANES // head_size
    lane_head = lax.broadcasted_iota(jnp.int32, (BLOCK, LANES), 1) // head_size
    pick_lane = lax.broadcasted_iota(jnp.int32, (BLOCK, LANES), 1)
    top_sum = jnp.zeros((mid, mid), f32)
    low_sum = jnp.zeros((mid, BLOCK), f32)
    top_cross = jnp.zeros((mid, LANES), f32)
    low_cross = jnp.zeros((mid, LANES), f32)
    all_cross = jnp.zeros((BLOCK, LANES), f32)
    within = []
    for first in range(0, head_share, pair):
        at = first * head_size
        grads = grad_low[:, at : at + LANES]
        values = stepped_low[:, at : at + LANES]
        total = None
        for k in range(pair):
            top, low = decay_strips(cum, cum_t, first + k)
            own = jnp.where(lane_head == k, grads, jnp.zeros_like(grads))
            pick = (pick_lane == first + k).astype(bf16)
            top_products = dot(own[:mid], values[:mid], 1, 1) * top
            low_products = dot(own[mid:], values, 1, 1) * low
            top_sum = top_sum + top_products
            low_sum = low_sum + low_products
            low_term = dot((low * low_scores).astype(bf16), grads[mid:], 0, 0)
            top_term = dot((top * top_scores).astype(bf16), grads[:mid], 0, 0)
            term = low_term + jnp.concatenate([top_term, jnp.zeros_like(top_term)], axis=0)
            total = term if k == 0 else jnp.where(lane_head == k, term, total)
            top_pairs = (top_products * top_scores).astype(bf16)
            low_pairs = (low_products * low_scores).astype(bf16)
            top_cross = top_cross + dot(top_pairs, pick[:mid]) - dot(top_pairs, pick[:mid], 0, 0)
            low_cross = low_cross + dot(low_pairs, pick)
            all_cross = all_cross + dot(low_pairs, pick[mid:], 0, 0)
        within.append(total)
    zeros = jnp.zeros((mid, mid), f32)
    gathered = jnp.concatenate([jnp.concatenate([top_sum, zeros], axis=1), low_sum], axis=0)
    gathered_low = jnp.where(lower, gathered, 0.0).astype(bf16)
    grad_b = grad_b + dot(gathered_low, c, 0, 0)
    grad_c = grad_c + dot(gathered_low, b)
    crossing = jnp.concatenate([top_cross, low_cross], axis=0) - all_cross

    by_x = jnp.concatenate(within, axis=1) + from_later
    fold = lambda values: dot(values.astype(bf16), spread, 1, 1)
    direct = fold(by_x * x)
    into = fold(grad_decayed * carried)
    onward = steps * fold(from_later * x)
    tops = jnp.sum(later * old, axis=0, keepdims=True) * jnp.exp(last)
    spanning = fold(jnp.broadcast_to(tops, (8, inner)))[0:1, :]
    upper = (row <= col).astype(bf16)
    strict = (row > col).astype(bf16)
    by_decay = select_rows(upper, into + crossing, 3) + select_rows(strict, onward, 2) + spanning
    by_step = direct + rate_ref[...] * by_decay
    grad_step = by_step * jax.nn.sigmoid(step_pre)
    small_ref[0:1, :] += jnp.sum(grad_step, axis=0, keepdims=True)
    small_ref[1:2, :] += jnp.sum(steps * by_decay, axis=0, keepdims=True)
    skips = jnp.sum(grad * x, axis=0, keepdims=True)
    small_ref[2:3, :] += sum(
        dot(term, spread, 1, 1) for term in split(jnp.broadcast_to(skips, (8, inner)), 2)
    )[0:1, :]

    def conv_back(buf, tail, by_pre, values, taps_ref, sums):
        buf[0:BLOCK, :] = by_pre
        buf[BLOCK:, :] = tail[...]
        tail[...] = by_pre[0:8, :]
        total = taps_ref[3:4, :] * by_pre
        sums[3:4, :] += jnp.sum(by_pre * values, axis=0, keepdims=True)
        sums[4:5, :] += jnp.sum(by_pre, axis=0, keepdims=True)
        for tap in range(CONV_WIDTH - 1):
            ahead = CONV_WIDTH - 1 - tap
            moved = buf[ahead : ahead + BLOCK, :]
            total = total + taps_ref[tap : tap + 1, :] * moved
            sums[tap : tap + 1, :] += jnp.sum(moved * values, axis=0, keepdims=True)
        return total.astype(bf16)

    by_conv = steps_x * by_x + skip_ref[...] * grad
    by_pre = by_conv * silu_slope(x_pre_ref[...].astype(f32))
    late_ref[:, :inner] = conv_back(
        x_buf, x_tail, by_pre, inner_ref[...].astype(f32), x_taps_ref, x_sums
    )
    by_state = jnp.concatenate([grad_b, grad_c], axis=1) * silu_slope(s_pre_ref[...].astype(f32))
    grad_state = conv_back(
        s_buf, s_tail, by_state, state_in_ref[...].astype(f32), s_taps_ref, s_sums
    )
    late_ref[:, inner : inner + 2 * half] = grad_state
    width = half // 2
    first = lax.broadcasted_iota(jnp.int32, (BLOCK, half), 1) < width
    left, right = grad_state[:, :half], grad_state[:, half:]
    turn = lambda v: jnp.concatenate([v[:, width:], v[:, :width]], axis=1)
    even, odd = jnp.where(first, left, turn(right)), jnp.where(first, turn(left), right)
    own_first, low_side = me_ref[2] == 0, me_ref[1] < 2
    for core, (one, other) in enumerate(((even, odd), (odd, even))):
        half_of = jnp.where(own_first, one, other)
        turned = turn(half_of)
        for side, part in enumerate((jnp.where(low_side, half_of, turned), jnp.where(low_side, turned, half_of))):
            if joined:
                part = jnp.where(first, part, turn(upper_parts[core + 2 * side]))
            s_parts[core + 2 * side] = part
    late_ref[:, inner + 2 * half :] = grad_step.astype(bf16)


def backward_scan(me, part, rows, starts, consts, carry, upper, head_share, head_size):
    first, stop = part
    count, inner = rows[0].shape
    state2 = rows[6].shape[1]
    wide = inner + state2 + LANES
    per = lambda width: pl.BlockSpec((BLOCK, width), lambda i: (stop - 1 - i, 0))
    joined = [] if upper is None else list(upper)[::-1]
    sizes = (head_share, head_size, LEN // BLOCK, stop - 1, len(joined))
    state_parts = pl.BlockSpec((4, BLOCK, state2 // 2), lambda i: (0, stop - first - 1 - i, 0))
    results = pl.pallas_call(
        functools.partial(backward_kernel, sizes),
        grid=(stop - first,),
        in_specs=[scalar_spec()]
        + [per(a.shape[1]) for a in rows]
        + [pl.BlockSpec((1, state2 // 2, inner), lambda i: (stop - 1 - i, 0, 0))]
        + [const_spec(a) for a in (*consts, *carry)]
        + ([state_parts, pl.BlockSpec(memory_space=pl.ANY)] if joined else []),
        out_specs=[per(wide)]
        + [state_parts]
        + [const_spec(a) for a in carry],
        out_shape=[out((count, wide), bf16)]
        + [out((4, (stop - first) * BLOCK, state2 // 2), bf16)]
        + [out(a.shape, f32) for a in carry],
        input_output_aliases={len(rows) + 3 + len(consts) + len(carry): 0} if joined else {},
        scratch_shapes=[
            pltpu.VMEM((BLOCK + 8, inner), f32),
            pltpu.VMEM((BLOCK + 8, state2), f32),
        ],
        compiler_params=params(),
        cost_estimate=cost(12),
    )(me, *rows, starts, *consts, *carry, *joined)
    return results[0], results[1], tuple(results[2:])


def late_kernel(sizes, me_ref, *refs):
    a_rels, b_rels, inner, half = sizes
    late_ref, *state_refs, normed_ref, a_send, a_keep, b_send, b_keep, total = refs

    @pl.when(pl.program_id(0) == 0)
    def _():
        total[...] = jnp.zeros(total.shape, f32)

    rest = inner + 2 * half
    width = LANES // 2
    turn = lambda v: jnp.concatenate([v[:, width:], v[:, :width]], axis=1)
    steps = turn(late_ref[:, rest:])
    state = sum(ref[...].astype(f32) for ref in state_refs).astype(bf16)
    state = jnp.where(pl.program_id(0) < pl.num_programs(0) // 2, state, turn(state))
    first = lax.broadcasted_iota(jnp.int32, (ROWS, LANES), 1) < width
    both = jnp.concatenate([late_ref[:, :inner], jnp.where(first, state, steps)], axis=1)
    total[...] += dot(normed_ref[...], both, 0, 0)

    @pl.when(pl.program_id(0) == pl.num_programs(0) - 1)
    def _():
        size, cut = a_send.shape[1:]
        for rels, send, keep, columns in (
            (a_rels, a_send, a_keep, slice(0, cut)),
            (b_rels, b_send, b_keep, slice(cut, None)),
        ):
            for to, found in zip((send, keep), rels):
                for i, rel in enumerate(found):
                    to[i] = total[row_of(me_ref[0] ^ rel, size), columns].astype(bf16)


def late_grads(me, late, states, normed, inner, half, shards, a_rels, b_rels):
    count, wide = late.shape
    features = normed.shape[1]
    size = features // shards
    cut = inner // 2
    per = lambda width: pl.BlockSpec((ROWS, width), lambda i: (i, 0))
    packed = pl.BlockSpec((ROWS, LANES), lambda i: (i % (count // ROWS // 2), 0))
    a_part, b_part = (shards // 2, size, cut), (shards // 2, size, inner + LANES - cut)
    outs = [a_part, a_part, b_part, b_part]
    return pl.pallas_call(
        functools.partial(late_kernel, (a_rels, b_rels, inner, half)),
        grid=(count // ROWS,),
        in_specs=[scalar_spec(), per(wide)] + [packed] * len(states) + [per(features)],
        out_specs=[pl.BlockSpec(dims, lambda i: (0, 0, 0)) for dims in outs],
        out_shape=[out(dims, bf16) for dims in outs],
        scratch_shapes=[pltpu.VMEM((features, inner + LANES), f32)],
        compiler_params=params(),
        cost_estimate=cost(5),
    )(me, late, *states, normed)


def rows_kernel(groups, me_ref, *refs):
    piece_refs, refs = refs[:groups], refs[groups:]
    late_ref, gate_grad_ref, scale_ref, z_ref, weight_ref, gain_ref = refs[:6]
    rows_send, rows_keep, gain_grad_ref, stat_ref = refs[6:]
    share = piece_refs[0].shape[1]

    @pl.when(pl.program_id(0) == 0)
    def _():
        gain_grad_ref[...] = jnp.zeros(gain_grad_ref.shape, f32)

    grad_gate = gate_grad_ref[...]
    late = late_ref[...]
    scale = scale_ref[:, 0:1]
    stat = jnp.zeros((ROWS, share), f32)
    for rel in range(groups):
        rows = row_of(me_ref[0 + 1] ^ rel, share)
        part = dot(grad_gate, z_ref[rows, :], 1, 1) + dot(late, weight_ref[rows, :], 1, 1)
        to = rows_send if rel % 2 else rows_keep
        to[rel // 2] = part.astype(bf16)
        product = piece_refs[rel][...].astype(f32) * scale * part
        gain_grad_ref[0:1, rows] += jnp.sum(product, axis=0, keepdims=True)
        stat = stat + product * gain_ref[:, rows]
    stat_ref[...] = row_sums(stat)


def row_grads(me, pieces, late, grad_gate, scale, z_all, weight, gain):
    count, share = pieces[0].shape
    groups = len(pieces)
    features = share * groups
    per = lambda width: pl.BlockSpec((ROWS, width), lambda i: (i, 0))
    parts = pl.BlockSpec((groups // 2, ROWS, share), lambda i: (0, i, 0))
    return pl.pallas_call(
        functools.partial(rows_kernel, groups),
        grid=(count // ROWS,),
        in_specs=[scalar_spec()]
        + [per(a.shape[1]) for a in (*pieces, late, grad_gate, scale)]
        + [const_spec(a) for a in (z_all, weight, gain)],
        out_specs=[
            parts,
            parts,
            pl.BlockSpec((8, features), lambda i: (0, 0)),
            pl.BlockSpec((8, ROWS), lambda i: (0, i)),
        ],
        out_shape=[
            out((groups // 2, count, share), bf16),
            out((groups // 2, count, share), bf16),
            out((8, features), f32),
            out((8, count), f32),
        ],
        compiler_params=params(),
        cost_estimate=cost(6),
    )(me, *pieces, late, grad_gate, scale, z_all, weight, gain)


def swap(value, axis, step):
    count = lax.axis_size(axis)
    return lax.ppermute(value, axis, [(i, i ^ step) for i in range(count)])


def steps_of(axis):
    found = []
    while 2 ** len(found) < lax.axis_size(axis):
        found.append(2 ** len(found))
    return found


def rels_of(order):
    rels = [0]
    for step in order:
        rels = rels + [rel ^ step for rel in rels]
    return rels


def halves_of(order):
    rels = rels_of(order[:0:-1])
    return [rel ^ order[0] for rel in rels], rels


def gather_steps(value, axis, order):
    held = value[None]
    for i, step in enumerate(order):
        held, got = yield held, swap(held, axis, step)
        if i < len(order) - 1:
            held = jnp.concatenate([held, got], axis=0)


def reduce_steps(send, keep, axis, order):
    for i, step in enumerate(order):
        keep, got = yield keep, swap(send, axis, step)
        if i < len(order) - 1:
            total = keep.astype(f32) + got.astype(f32)
            mid = total.shape[0] // 2
            keep, send = total[:mid], total[mid:].astype(bf16)


def pair_steps(send, keep, axis, order):
    keep, got = yield keep, swap(send, axis, order[0])
    send = (keep[1:].astype(f32) + got[1:].astype(f32)).astype(bf16)
    yield (keep, got), swap(send, axis, order[1])


def sum_steps(value, axis, order):
    for step in order:
        value, got = yield value, swap(value, axis, step)
        value = value + got


class Exchange:
    def __init__(self, steps, left=0):
        self.steps, self.value, self.ended, self.left = steps, None, False, left

    def advance(self):
        self.left -= 1
        try:
            self.value = self.steps.send(self.value)
        except StopIteration:
            self.ended = True

    def total(self):
        keep, got = self.value
        return keep.astype(f32) + got.astype(f32)


def phase(exchanges, beside=()):
    values, beside = lax.optimization_barrier(([e.value for e in exchanges], beside))
    for exchange, value in zip(exchanges, values):
        exchange.value = value
    return beside


def finish(exchanges, jobs):
    moving, results = exchanges, [None] * len(jobs)
    while moving:
        for exchange in moving:
            exchange.advance()
        moving = [exchange for exchange in moving if not exchange.ended]
        new = [i for i, job in enumerate(jobs) if job[0].ended and results[i] is None]
        made = [jobs[i][1]() for i in new]
        if any(exchange.left > 0 for exchange in moving):
            made = phase(moving, made)
        for i, result in zip(new, made):
            results[i] = result
    return results


def body(
    tokens,
    z_weight,
    x_weight,
    bc_weight,
    dt_weight,
    out_weight,
    norm_gain,
    gate_gain,
    x_conv_weight,
    x_conv_bias,
    bc_conv_weight,
    bc_conv_bias,
    step_bias,
    decay_log,
    skip_gain,
    cotangent,
):
    head_index = lax.axis_index("heads")
    shard_index = lax.axis_index("shard")
    groups = lax.axis_size("heads")
    shards = lax.axis_size("shard")
    row_count, feature_share = tokens.shape
    feature_total = feature_share * groups
    size, inner_share = z_weight.shape
    head_share = dt_weight.shape[1]
    head_size = inner_share // head_share
    state_width = bc_weight.shape[1]
    half = state_width // 2
    near = steps_of("shard")
    far = near[::-1]
    rels = rels_of(far)
    core = head_index % 2
    me = jnp.stack([shard_index, head_index, core]).astype(jnp.int32)
    step_pad = LANES - head_share

    own_half = lax.dynamic_slice_in_dim(bc_weight, core * half, half, 1)
    scan_weight = jnp.concatenate(
        [x_weight, own_half, jnp.pad(dt_weight, ((0, 0), (0, step_pad)))], axis=1
    )
    o_order = near[:1] + far[:-1]
    scan_x = Exchange(gather_steps(scan_weight, "shard", far))
    z_x = Exchange(gather_steps(z_weight, "shard", far))
    o_x = Exchange(gather_steps(out_weight.T, "shard", o_order), len(far))
    last = len(far) - 1
    cut = lambda v: v[:, :, inner_share : inner_share + half]
    for i in range(len(far)):
        scan_x.advance()
        moving = [scan_x]
        if i > 0:
            z_x.advance()
            moving.append(z_x)
        if i != 1:
            o_x.advance()
            moving.append(o_x)
        if i == 0:
            beside = (swap(tokens, "heads", 2), swap(tokens, "heads", 1))
            tokens_across, tokens_near, z_from, cot_from = phase(
                moving, (*beside, z_weight, cotangent)
            )
            z_x = Exchange(gather_steps(z_from, "shard", far), len(far))
        elif i == last:
            beside = (
                swap(tokens_across, "heads", 1),
                swap(cot_from, "heads", 2),
                swap(cut(scan_x.value[0]), "heads", 1),
            )
            tokens_last, cot_across, other_held = phase(moving, beside)
        else:
            (cot_from,) = phase(moving, (cot_from,))
    scan_held, scan_got = scan_x.value
    token_parts = [tokens, tokens_near, tokens_across, tokens_last]
    other_got = swap(cut(scan_got), "heads", 1)

    pad_lanes = lambda v: jnp.pad(v, (0, step_pad))[None]
    rate = pad_lanes(-jnp.exp(decay_log))
    skip_x = jnp.repeat(skip_gain, head_size)[None]
    z_x.advance()
    o_x.advance()
    cot_near, cot_last = swap(cot_from, "heads", 1), swap(cot_across, "heads", 1)
    scan = forward_scan(
        me,
        token_parts,
        (scan_held, scan_got, other_held, other_got),
        (
            norm_gain[None],
            x_conv_weight,
            x_conv_bias[None],
            bc_conv_weight,
            bc_conv_bias[None],
            pad_lanes(step_bias),
            rate,
            skip_x,
        ),
        head_share,
        head_size,
        rels,
    )

    (
        normed,
        scale_in,
        inner_in,
        x_pre,
        x,
        state_in,
        s_pre,
        bc,
        step_pre,
        cum,
        starts,
        scanned,
        scan_weight_all,
    ), (cot_near, cot_last) = phase([z_x, o_x], (scan, (cot_near, cot_last)))
    finish([z_x, o_x], [])
    cot_parts = [cotangent, cot_near, cot_across, cot_last]

    gain_row = gate_gain[None]
    gate_in, grad_mid, stats, z_all, o_all = gate(
        me, cot_parts, (*z_x.value, *o_x.value), normed, scanned, gain_row, rels, rels_of(o_order)
    )
    for step in (1, 2):
        stats = stats + swap(stats, "heads", step)

    send_rels, keep_rels = halves_of(near)
    o_sums = near[1:] + near[:1]
    (
        grad_scanned,
        grad_gate,
        out_send,
        out_keep,
        z_send,
        z_keep,
        o_send,
        o_keep,
        gate_gain_grad,
    ) = mix(
        me, cot_parts, stats, normed, gate_in, grad_mid, scanned, o_all, gain_row,
        shards, (send_rels, keep_rels), halves_of(o_sums),
    )
    z_x = Exchange(reduce_steps(z_send, z_keep, "shard", near), len(near))
    o_x = Exchange(reduce_steps(o_send, o_keep, "shard", o_sums), len(near))
    out_x = Exchange(reduce_steps(out_send, out_keep, "heads", [1, 2]))

    blocks = row_count // BLOCK
    carry = tuple(
        jnp.zeros(dims, f32)
        for dims in (
            (8, inner_share),
            (8, state_width),
            (8, LANES),
            (8, inner_share),
            (8, state_width),
            (half, inner_share),
        )
    )
    scan_rows = (grad_scanned, inner_in, x_pre, x, state_in, s_pre, bc, step_pre, cum)
    scan_consts = (x_conv_weight, bc_conv_weight, rate, skip_x)
    sizes = (head_share, head_size)
    quarter = half // 2
    for exchange in (z_x, o_x, out_x):
        exchange.advance()
    late, s_upper, carry = phase(
        [z_x, o_x, out_x],
        backward_scan(me, (blocks // 2, blocks), scan_rows, starts, scan_consts, carry, None, *sizes),
    )
    for exchange in (z_x, o_x, out_x):
        exchange.advance()
    late, state_parts, carry = phase(
        [z_x, o_x, out_x],
        backward_scan(
            me, (0, blocks // 2), scan_rows, starts, scan_consts, carry, (late, s_upper), *sizes
        ),
    )
    x_sums, s_sums, small = carry[:3]
    (rows_send, rows_keep, gain_grad, stat), state_got = phase(
        [],
        (
            row_grads(
                me, token_parts, late, grad_gate, scale_in, z_all, scan_weight_all, norm_gain[None]
            ),
            [swap(state_parts[step], "heads", step) for step in (1, 2, 3)],
        ),
    )

    b_sums = near[1:] + near[:1]
    rows_x = Exchange(pair_steps(rows_send, rows_keep, "heads", [1, 2]))
    by_heads = jnp.concatenate([gain_grad[0], stat[0], s_sums[: CONV_WIDTH + 1].reshape(-1)])
    rows_x.advance()
    (a_send, a_keep, b_send, b_keep), by_heads, got = phase(
        [rows_x, z_x, o_x],
        (
            late_grads(
                me, late, (state_parts[0], *state_got), normed, inner_share, half, shards, halves_of(near), halves_of(b_sums)
            ),
            by_heads,
            [swap(by_heads, "heads", step) for step in (1, 2, 3)],
        ),
    )
    a_x = Exchange(reduce_steps(a_send, a_keep, "shard", near), len(near))
    b_x = Exchange(reduce_steps(b_send, b_keep, "shard", b_sums), len(near))
    by_heads = (by_heads + got[0]) + (got[1] + got[2])
    local = jnp.concatenate(
        [
            gate_gain_grad[0],
            x_sums[: CONV_WIDTH + 1].reshape(-1),
            small[0, :head_share],
            small[1, :head_share],
            small[2, :head_share],
        ]
    )
    summed = jnp.concatenate(
        [
            lax.dynamic_slice_in_dim(by_heads, head_index * feature_share, feature_share, 0),
            by_heads[feature_total + row_count :],
            local,
        ]
    )
    small_x = Exchange(sum_steps(summed, "shard", near), len(near))
    for exchange in (a_x, b_x, rows_x, small_x, z_x):
        exchange.advance()
    mixed = (tokens.astype(f32) + out_x.total()[0]).astype(bf16)
    norm_stat = by_heads[feature_total : feature_total + row_count]
    mixed, norm_stat = phase([a_x, b_x, rows_x, small_x, z_x], (mixed, norm_stat))
    scale = scale_in[:, :1]
    gain_share = lax.dynamic_slice_in_dim(norm_gain, head_index * feature_share, feature_share, 0)

    def token_grads():
        tokens_hat = tokens.astype(f32) * scale
        (first, second), third = rows_x.value
        total = first[0].astype(f32) + second[0].astype(f32) + third[0].astype(f32)
        scaled = total * gain_share - tokens_hat * (norm_stat / feature_total)[:, None]
        return (cotangent.astype(f32) + scale * scaled).astype(bf16)

    tokens_grad, z_sum, o_sum, a_sum, b_sum, summed = finish(
        [o_x, a_x, b_x, rows_x, small_x, z_x],
        [
            (rows_x, token_grads),
            (z_x, lambda: z_x.total()[0]),
            (o_x, lambda: o_x.total()[0].T),
            (a_x, lambda: a_x.total()[0]),
            (b_x, lambda: b_x.total()[0]),
            (small_x, small_x.total),
        ],
    )
    steps_at = inner_share - a_sum.shape[1]

    cuts, at = [], 0
    taps = CONV_WIDTH + 1
    for count in (feature_share, taps * state_width, inner_share, taps * inner_share) + (head_share,) * 3:
        cuts.append(summed[at : at + count])
        at += count
    bc_taps = cuts[1].reshape(taps, state_width)
    x_taps = cuts[3].reshape(taps, inner_share)
    return (
        mixed,
        tokens_grad,
        z_sum,
        jnp.concatenate([a_sum, b_sum[:, :steps_at]], axis=1),
        b_sum[:, steps_at : steps_at + quarter],
        b_sum[:, steps_at + LANES // 2 : steps_at + LANES // 2 + head_share],
        o_sum,
        cuts[0],
        cuts[2],
        x_taps[:CONV_WIDTH],
        x_taps[CONV_WIDTH],
        bc_taps[:CONV_WIDTH],
        bc_taps[CONV_WIDTH],
        cuts[4],
        cuts[5] * rate[0, :head_share],
        cuts[6],
    )


def solution(mesh):
    placed = (
        P("shard", "heads"),
        P("shard", "heads"),
        P("shard", "heads"),
        P("shard", None),
        P("shard", "heads"),
        P("heads", "shard"),
        P(),
        P("heads"),
        P(None, "heads"),
        P("heads"),
        P(),
        P(),
        P("heads"),
        P("heads"),
        P("heads"),
        P("shard", "heads"),
    )
    return jax.shard_map(
        body,
        mesh=mesh,
        in_specs=placed,
        out_specs=(
            P("shard", "heads"),
            P("shard", "heads"),
            P("shard", "heads"),
            P("shard", "heads"),
            P("shard", "heads"),
            P("shard", "heads"),
            P("heads", "shard"),
            P("heads"),
            P("heads"),
            P(None, "heads"),
            P("heads"),
            P(),
            P(),
            P("heads"),
            P("heads"),
            P("heads"),
        ),
        check_vma=False,
    )
```
